512 devices in a mesh: dp: 16 (over y, x_hi, core), seq: 16 (over z), kv: 2 (over x_lo).
Axes of the slice: x: 4 (x_hi: 2, x_lo: 2; x = x_hi * 2 + x_lo), y: 4, z: 16, core: 2. Of those that a mesh axis runs over, the one named last changes fastest.
Arguments:
- slab_queries: bfloat16 [16, 768, 1152], P('dp', 'seq'), may hold values from -16 to 16
- key_tokens: bfloat16 [16, 8192, 1152], P('dp', ('seq', 'kv')), may hold values from -16 to 16
- value_tokens: bfloat16 [16, 8192, 1152], P('dp', ('seq', 'kv')), may hold values from -6 to 6
- grad_output: bfloat16 [16, 768, 1152], P('dp'), may hold values from -6 to 6
- out_weight: bfloat16 [1152, 1152], P('seq'), may hold values from -0.1875 to 0.1875
Outputs:
- grad_keys: bfloat16 [16, 8192, 1152], P('dp', ('seq', 'kv'))
- grad_values: bfloat16 [16, 8192, 1152], P('dp', ('seq', 'kv'))
- grad_queries: bfloat16 [16, 768, 1152], P('dp', ('seq', 'kv'))
- grad_weight: float32 [1152, 1152], P('seq', ('dp', 'kv'))
The draws below stay inside these ranges and needn't reach their ends.
All inputs are finite; a program needn't handle non-finite values.
Results may differ from the reference program's by a relative error of at most 0.02.
Values may be sent and summed in bfloat16 or wider, within the bound.
No kernel may reach another device: no remote copies, remote signals or barrier semaphores. Data moves between devices by JAX's collectives and lax.ppermute only.
A program may use at most 128 MiB of HBM per device.

```python
import math
import jax
import jax.numpy as jnp
from jax import lax

D = 1152
HEADS = 16
HD = 72
ROWS = 768
SEQ = 8192
IMAGES = 16


def shared_direction(key):
    return jax.random.rademacher(key, (D,), jnp.float32)


def query_strengths():
    targets = jnp.array([110.0, 140.0, 160.0, 220.0, 260.0, 300.0], jnp.float32)
    return jnp.minimum(targets / (12.0 * math.sqrt(HD)), 15.0)


def draw_slab_queries(key, part):
    direction = shared_direction(key)
    key = jax.random.fold_in(key, 11)
    strengths = query_strengths()
    sample = jnp.clip(jax.random.normal(key, (IMAGES, ROWS, D), jnp.float32), -6.0, 6.0)
    sample = sample.at[:, 0:6, :].set(strengths[None, :, None] * direction[None, None, :])
    return sample.astype(jnp.bfloat16)


def draw_key_tokens(key, part):
    direction = shared_direction(key)
    key = jax.random.fold_in(key, 23)
    sample = jnp.clip(3.0 * jax.random.normal(key, (IMAGES, SEQ, D), jnp.float32), -12.0, 12.0)
    sample = sample.at[:, 5, :].set(12.0 * direction[None, :])
    sample = sample.at[:, SEQ // 2 + 7, :].set(11.92 * direction[None, :])
    return sample.astype(jnp.bfloat16)


def raised(result, own_key, source, target, blocks, factor):
    def block_of(position):
        return (jnp.arange(result.shape[position]) // (result.shape[position] // blocks)).reshape((-1,) + (1,) * (result.ndim - 1 - position))

    one_side = jax.random.permutation(own_key, blocks)[block_of(target)]
    second = (block_of(target) + blocks // 2) % blocks
    return jnp.where((block_of(source) == one_side) | (block_of(source) == second), factor * result, result)


def shard_levels(stream_key, dims, cuts, smallest, high):
    factor_of = 1.0
    for dim, blocks in cuts:
        draws = jax.random.uniform(jax.random.fold_in(jax.random.fold_in(stream_key, 6), dim), (blocks,), jnp.float32, smallest / len(cuts), high / len(cuts))
        factor_of = factor_of * jnp.repeat(jnp.exp(draws), dims[dim] // blocks).reshape((-1,) + (1,) * (len(dims) - 1 - dim))
    return factor_of


def gaussian(key, shape, deviation, reach, split=(), held_as=jnp.bfloat16):
    drawn = deviation * jax.random.normal(key, shape, jnp.float32)
    if split:
        drawn = drawn * shard_levels(key, shape, split, -0.22, 0.18)
    return jnp.clip(drawn, -reach, reach).astype(held_as)


def heavy_noise(key, dims, deviation, limit, pieces, heavy, kind=jnp.bfloat16):
    entries = deviation * jax.random.normal(key, dims, jnp.float32)
    if pieces:
        entries = entries * shard_levels(key, dims, pieces, -0.22, 0.18)
    return jnp.clip(raised(entries, jax.random.fold_in(key, 3), *heavy), -limit, limit).astype(kind)


def setup_inputs(seed: int = 0) -> dict:
    splits = jax.random.split(jax.random.key(seed), 6)
    return {
        "slab_queries": draw_slab_queries(jax.random.fold_in(splits[5], 71), 0),
        "key_tokens": draw_key_tokens(jax.random.fold_in(splits[5], 71), 0),
        "value_tokens": gaussian(splits[2], (IMAGES, SEQ, D), 1.0, 6.0, ((0, 16), (1, 32))),
        "grad_output": heavy_noise(splits[3], (IMAGES, ROWS, D), 1.0, 6.0, ((0, 16),), (0, 2, 16, 2.0)),
        "out_weight": gaussian(splits[4], (D, D), D ** -0.5, 0.1875, ((0, 16),)),
    }


def head_grads(query_img, key_img, value_img, grad_img, out_weight, head_index):
    offset = (head_index * HD).astype(jnp.int32)
    query_head = lax.dynamic_slice_in_dim(query_img, offset, HD, 1)
    key_head = lax.dynamic_slice_in_dim(key_img, offset, HD, 1)
    value_head = lax.dynamic_slice_in_dim(value_img, offset, HD, 1)
    weight_rows = lax.dynamic_slice_in_dim(out_weight, offset, HD, 0)
    factor = 1.0 / math.sqrt(HD)
    grad_head = jnp.dot(grad_img, weight_rows.T, preferred_element_type=jnp.float32).astype(jnp.bfloat16)
    logits = jnp.dot(query_head, key_head.T, preferred_element_type=jnp.float32) * factor
    highest = lax.optimization_barrier(jnp.max(logits, axis=1, keepdims=True))
    weights = jnp.exp(logits - highest)
    totals = lax.optimization_barrier(jnp.sum(weights, axis=1, keepdims=True))
    upstream = jnp.dot(grad_head, value_head.T, preferred_element_type=jnp.float32)
    delta_rows = lax.optimization_barrier(jnp.sum(weights * upstream, axis=1, keepdims=True)) / totals
    probabilities = weights / totals
    probs_low = probabilities.astype(jnp.bfloat16)
    attn_head = jnp.dot(probs_low, value_head, preferred_element_type=jnp.float32)
    grad_value = jnp.dot(probs_low.T, grad_head, preferred_element_type=jnp.float32).astype(jnp.bfloat16)
    grad_scores = (probabilities * (upstream - delta_rows)).astype(jnp.bfloat16)
    grad_key = (jnp.dot(grad_scores.T, query_head, preferred_element_type=jnp.float32) * factor).astype(jnp.bfloat16)
    grad_query = jnp.dot(grad_scores, key_head, preferred_element_type=jnp.float32) * factor
    return (grad_key, grad_value, grad_query, attn_head)

def join_heads(stacked):
    return jnp.transpose(stacked, (1, 0, 2)).reshape(stacked.shape[1], D)

def reference(slab_queries, key_tokens, value_tokens, grad_output, out_weight):

    def one_image(image_index):
        query_img = slab_queries[image_index]
        key_img = key_tokens[image_index]
        value_img = value_tokens[image_index]
        grad_img = grad_output[image_index]

        def one_head(head_index):
            return head_grads(query_img, key_img, value_img, grad_img, out_weight, head_index)
        grad_key, grad_value, grad_query, attn_head = lax.map(one_head, jnp.arange(HEADS, dtype=jnp.int32))
        attn_rows = join_heads(attn_head)
        weight_term = jnp.dot(attn_rows.T, grad_img.astype(jnp.float32), precision=lax.Precision.HIGHEST, preferred_element_type=jnp.float32)
        return (join_heads(grad_key), join_heads(grad_value), join_heads(grad_query).astype(jnp.bfloat16), weight_term)
    grad_keys, grad_values, grad_queries, weight_terms = lax.map(one_image, jnp.arange(IMAGES, dtype=jnp.int32))
    return (grad_keys, grad_values, grad_queries, lax.optimization_barrier(jnp.sum(weight_terms, axis=0)))
```

```python
import math

import jax
import jax.numpy as jnp
from jax import lax
from jax.experimental import pallas as pl
from jax.experimental.pallas import tpu as pltpu
from jax.sharding import Mesh
from jax.sharding import PartitionSpec as P

HD = 72
ROWS = 768
FACTOR = 1.0 / math.sqrt(HD)
SCALE = FACTOR * math.log2(math.e)
BF = jnp.bfloat16
F32 = jnp.float32
CUBE = ("j", "kv")
DP = ("y", "xh", "core")
SEQ = ("t", "j")
PARAMS = pltpu.CompilerParams(vmem_limit_bytes=48 * 1024 * 1024)
PARAMS_SEQ = pltpu.CompilerParams(
    vmem_limit_bytes=48 * 1024 * 1024, dimension_semantics=("arbitrary",)
)


def heads_of(place):
    j, v = place // 2, place % 2
    return (8 * v + j, 8 * v + 4 + j)


def nn(a, b):
    return lax.dot_general(a, b, (((1,), (0,)), ((), ())), preferred_element_type=F32)


def pack_keys_kernel(k_ref, q_ref, o_ref):
    turned = k_ref[...].astype(F32).T
    rows = q_ref[...].astype(F32)
    for place in range(8):
        a, b = heads_of(place)
        o_ref[place, 0:144, :] = jnp.concatenate(
            [turned[HD * a : HD * a + HD], turned[HD * b : HD * b + HD]], axis=0
        ).astype(BF)
        qa = rows[:, HD * a : HD * a + HD]
        qb = rows[:, HD * b : HD * b + HD]
        middle = jnp.concatenate([qa[16:24], qb[0:8]], axis=0)
        o_ref[place, 144:160, :] = jnp.concatenate(
            [qa[0:16], middle, qb[8:24], jnp.zeros((16, 40), F32)], axis=1
        ).astype(BF)


def pack_values_kernel(v_ref, o_ref):
    turned = v_ref[...].astype(F32).T
    for place in range(8):
        a, b = heads_of(place)
        o_ref[place] = jnp.concatenate(
            [turned[HD * a : HD * a + HD], turned[HD * b : HD * b + HD]], axis=0
        ).astype(BF)


def unpack_kernel(g_ref, k_ref, v_ref):
    for part, o_ref in ((0, k_ref), (1, v_ref)):
        heads = [None] * 16
        for place in range(8):
            block = g_ref[place, 144 * part : 144 * part + 144, :].astype(F32)
            a, b = heads_of(place)
            heads[a] = block[0:HD]
            heads[b] = block[HD : 2 * HD]
        o_ref[...] = jnp.concatenate(heads, axis=0).T.astype(BF)


def first_kernel(kq_ref, v_ref, qg_ref, ga_ref, st_ref, ot_ref, q_ref, qs_ref, qt_ref):
    step = pl.program_id(0)

    @pl.when(step == 0)
    def _():
        for block in range(32):
            piece = qg_ref[block].astype(F32)
            base = 24 * block
            qs_ref[0, base : base + 16, :] = piece[:, 0:72]
            qs_ref[0, base + 16 : base + 24, :] = piece[0:8, 72:144]
            qs_ref[1, base : base + 8, :] = piece[8:16, 72:144]
            qs_ref[1, base + 8 : base + 24, :] = piece[:, 144:216]
        for h in range(2):
            q_ref[h] = qs_ref[h].astype(BF)
            qt_ref[h] = qs_ref[h].T.astype(BF)
        st_ref[0:2, :] = jnp.full((2, ROWS), -1e30, F32)
        st_ref[2:8, :] = jnp.zeros((6, ROWS), F32)
        ot_ref[...] = jnp.zeros_like(ot_ref)

    keys = kq_ref[0, 0:144, :].astype(F32)
    values = v_ref[0].astype(F32)
    for h in range(2):
        kh = keys[HD * h : HD * h + HD].T.astype(BF)
        vt = values[HD * h : HD * h + HD]
        vh = vt.T.astype(BF)
        s = nn(kh, qt_ref[h])
        u = nn(vh, ga_ref[h])
        before = st_ref[h : h + 1, :]
        highest = jnp.maximum(before, jnp.max(s, axis=0, keepdims=True))
        again = jnp.exp2((before - highest) * SCALE)
        e = jnp.exp2((s - highest) * SCALE)
        st_ref[h : h + 1, :] = highest
        st_ref[2 + h : 3 + h, :] = st_ref[2 + h : 3 + h, :] * again + jnp.sum(
            e, axis=0, keepdims=True
        )
        st_ref[4 + h : 5 + h, :] = st_ref[4 + h : 5 + h, :] * again + jnp.sum(
            e * u, axis=0, keepdims=True
        )
        ot_ref[h] = ot_ref[h] * again + nn(vt.astype(BF), e.astype(BF))


def joined(sg_ref, h):
    tops = [sg_ref[t, h : h + 1, :] for t in range(4)]
    highest = jnp.maximum(jnp.maximum(tops[0], tops[1]), jnp.maximum(tops[2], tops[3]))
    total = jnp.zeros((1, ROWS), F32)
    weighted = jnp.zeros((1, ROWS), F32)
    for t in range(4):
        part = jnp.exp2((tops[t] - highest) * SCALE)
        total = total + sg_ref[t, 2 + h : 3 + h, :] * part
        weighted = weighted + sg_ref[t, 4 + h : 5 + h, :] * part
    return highest, total, weighted / total


def weight_kernel(sg_ref, st_ref, ot_ref, go_ref, o_ref):
    rows = []
    for h in range(2):
        highest, total, _ = joined(sg_ref, h)
        share = jnp.exp2((st_ref[h : h + 1, :] - highest) * SCALE) / total
        rows.append(ot_ref[h] * share)
    attn = jnp.concatenate(rows, axis=0).astype(BF)
    o_ref[...] = nn(attn, go_ref[...]).T.astype(BF)


def second_kernel(
    kq_ref, v_ref, q_ref, ga_ref, sg_ref, kv_ref, dq_ref, qt_ref, gn_ref, stat_ref, dqt_ref
):
    step = pl.program_id(0)

    @pl.when(step == 0)
    def _():
        for h in range(2):
            qt_ref[h] = q_ref[h].astype(F32).T.astype(BF)
            gn_ref[h] = ga_ref[h].astype(F32).T.astype(BF)
            highest, total, delta = joined(sg_ref, h)
            stat_ref[h : h + 1, :] = highest
            stat_ref[2 + h : 3 + h, :] = 1.0 / total
            stat_ref[4 + h : 5 + h, :] = delta
        dqt_ref[...] = jnp.zeros_like(dqt_ref)

    keys = kq_ref[0, 0:144, :].astype(F32)
    values = v_ref[0].astype(F32)
    for h in range(2):
        kt = keys[HD * h : HD * h + HD]
        kh = kt.T.astype(BF)
        vh = values[HD * h : HD * h + HD].T.astype(BF)
        s = nn(kh, qt_ref[h])
        u = nn(vh, ga_ref[h])
        p = jnp.exp2((s - stat_ref[h : h + 1, :]) * SCALE) * stat_ref[2 + h : 3 + h, :]
        ds = (p * (u - stat_ref[4 + h : 5 + h, :])).astype(BF)
        dv = nn(p.astype(BF), gn_ref[h])
        dk = nn(ds, q_ref[h]) * FACTOR
        dqt_ref[HD * h : HD * h + HD, :] += nn(kt.astype(BF), ds)
        if h == 0:
            dk0, dv0 = dk, dv
    kv_ref[0, 0:144, :] = jnp.concatenate([dk0.T, dk.T], axis=0).astype(BF)
    kv_ref[0, 144:288, :] = jnp.concatenate([dv0.T, dv.T], axis=0).astype(BF)

    @pl.when(step == pl.num_programs(0) - 1)
    def _():
        dq_ref[...] = (dqt_ref[...] * FACTOR).T.astype(BF)


def whole(*shape):
    return pl.BlockSpec(shape, lambda i: (0,) * len(shape))


def block(*shape):
    return pl.BlockSpec((1,) + shape, lambda i: (i,) + (0,) * len(shape))


def on_device(slab_queries, key_tokens, value_tokens, grad_output, out_weight):
    query_rows = slab_queries[0]
    key_rows = key_tokens[0]
    value_rows = value_tokens[0]
    cotangent = grad_output[0]
    t = lax.axis_index("t")
    v = lax.axis_index("kv")
    swap = [(0, 1), (1, 0)]

    query_half = lax.dynamic_slice_in_dim(query_rows, 24 * v, 24, 0)
    packed_keys = pl.pallas_call(
        pack_keys_kernel,
        out_shape=jax.ShapeDtypeStruct((8, 160, 256), BF),
        compiler_params=PARAMS,
        name="pack_keys",
    )(key_rows, query_half)
    keys = lax.all_to_all(packed_keys, CUBE, 0, 0, tiled=True)

    cotangent_half = lax.dynamic_slice_in_dim(cotangent, 384 * v, 384, 0)
    grad_half = lax.dot_general(
        out_weight, cotangent_half, (((1,), (1,)), ((), ())), preferred_element_type=F32
    ).astype(BF)
    grad_four = lax.all_gather(grad_half, "t")
    grad_keep = lax.dynamic_slice_in_dim(grad_four, 2 * v, 2, 0)
    grad_sent = lax.dynamic_slice_in_dim(grad_four, 2 - 2 * v, 2, 0)
    grad_come = lax.ppermute(grad_sent, "kv", swap)
    grad_heads = jnp.where(
        v == 0,
        jnp.concatenate([grad_keep, grad_come], axis=2),
        jnp.concatenate([grad_come, grad_keep], axis=2),
    )

    packed_values = pl.pallas_call(
        pack_values_kernel,
        out_shape=jax.ShapeDtypeStruct((8, 144, 256), BF),
        compiler_params=PARAMS,
        name="pack_values",
    )(value_rows)
    values = lax.all_to_all(packed_values, CUBE, 0, 0, tiled=True)

    query_pieces = lax.all_gather(keys[:, 144:160, :].reshape(128, 256), "t")
    query_pieces = query_pieces.reshape(32, 16, 256)

    stats, attn_turned, queries = pl.pallas_call(
        first_kernel,
        grid=(8,),
        in_specs=[block(160, 256), block(144, 256), whole(32, 16, 256), whole(2, HD, ROWS)],
        out_specs=[whole(8, ROWS), whole(2, HD, ROWS), whole(2, ROWS, HD)],
        out_shape=[
            jax.ShapeDtypeStruct((8, ROWS), F32),
            jax.ShapeDtypeStruct((2, HD, ROWS), F32),
            jax.ShapeDtypeStruct((2, ROWS, HD), BF),
        ],
        scratch_shapes=[pltpu.VMEM((2, ROWS, HD), F32), pltpu.VMEM((2, HD, ROWS), BF)],
        compiler_params=PARAMS_SEQ,
        name="first_pass",
    )(keys, values, query_pieces, grad_heads)

    gathered = lax.all_gather(stats, "t")

    weight_turned = pl.pallas_call(
        weight_kernel,
        out_shape=jax.ShapeDtypeStruct((1152, 144), BF),
        compiler_params=PARAMS,
        name="weight_part",
    )(gathered, stats, attn_turned, cotangent)
    weight_come = lax.all_to_all(weight_turned, DP, 0, 0, tiled=True)

    grads, query_grad = pl.pallas_call(
        second_kernel,
        grid=(8,),
        in_specs=[
            block(160, 256),
            block(144, 256),
            whole(2, ROWS, HD),
            whole(2, HD, ROWS),
            whole(4, 8, ROWS),
        ],
        out_specs=[block(288, 256), whole(ROWS, 144)],
        out_shape=[
            jax.ShapeDtypeStruct((8, 288, 256), BF),
            jax.ShapeDtypeStruct((ROWS, 144), BF),
        ],
        scratch_shapes=[
            pltpu.VMEM((2, HD, ROWS), BF),
            pltpu.VMEM((2, ROWS, HD), BF),
            pltpu.VMEM((8, ROWS), F32),
            pltpu.VMEM((144, ROWS), F32),
        ],
        compiler_params=PARAMS_SEQ,
        name="second_pass",
    )(keys, values, queries, grad_heads, gathered)

    query_sum = lax.psum_scatter(query_grad, "t", scatter_dimension=0, tiled=True)
    grads_back = lax.all_to_all(grads, CUBE, 0, 0, tiled=True)
    key_out, value_out = pl.pallas_call(
        unpack_kernel,
        out_shape=[jax.ShapeDtypeStruct((256, 1152), BF)] * 2,
        compiler_params=PARAMS,
        name="unpack_grads",
    )(grads_back)

    query_back = lax.all_to_all(query_sum, CUBE, 0, 0, tiled=True)
    query_out = (
        query_back.reshape(4, 2, 24, 2, HD).transpose(2, 1, 3, 0, 4).reshape(24, 1152)
    )

    weight_sum = jnp.sum(weight_come.astype(F32).reshape(16, HD, 144), axis=0)
    weight_all = jnp.sum(lax.all_gather(weight_sum, "t"), axis=0)
    weight_head = jnp.where(t % 2 == 0, weight_all[:, 0:HD], weight_all[:, HD : 2 * HD])
    weight_low, weight_high = weight_head[0:36], weight_head[36:72]
    weight_sent = jnp.where(v == 0, weight_high, weight_low)
    weight_keep = jnp.where(v == 0, weight_low, weight_high)
    weight_other = lax.ppermute(weight_sent, "kv", swap)
    weight_out = jnp.where(v == t // 2, weight_keep, weight_other).T
    return (key_out[None], value_out[None], query_out[None], weight_out)


def solution(mesh):
    cube = Mesh(mesh.devices.reshape(4, 2, 2, 4, 4, 2), DP + SEQ + ("kv",))
    return jax.shard_map(
        on_device,
        mesh=cube,
        in_specs=(
            P(DP, SEQ, None),
            P(DP, SEQ + ("kv",), None),
            P(DP, SEQ + ("kv",), None),
            P(DP, None, None),
            P(SEQ, None),
        ),
        out_specs=(
            P(DP, SEQ + ("kv",), None),
            P(DP, SEQ + ("kv",), None),
            P(DP, SEQ + ("kv",), None),
            P(SEQ, DP + ("kv",)),
        ),
        check_vma=False,
    )
```

```python
import math

import jax
import jax.numpy as jnp
from jax import lax
from jax.experimental import pallas as pl
from jax.experimental.pallas import tpu as pltpu
from jax.sharding import Mesh
from jax.sharding import PartitionSpec as P

HD = 72
ROWS = 768
FACTOR = 1.0 / math.sqrt(HD)
SCALE = FACTOR * math.log2(math.e)
BF = jnp.bfloat16
F32 = jnp.float32
VMEM = 60 * 1024 * 1024
LONG = pl.CostEstimate(flops=60_000_000_000, bytes_accessed=200_000_000, transcendentals=0)
ANY = pl.BlockSpec(memory_space=pl.ANY)
SCALAR = pl.BlockSpec(memory_space=pltpu.SMEM)
HERE = pl.BlockSpec(memory_space=pltpu.VMEM)
CUBE = ("j", "kv")
DP = ("y", "xh", "core")
SEQ = ("t", "j")
PARAMS = pltpu.CompilerParams(vmem_limit_bytes=VMEM)
PARAMS_SEQ = pltpu.CompilerParams(
    vmem_limit_bytes=VMEM, dimension_semantics=("arbitrary",)
)


def heads_of(place):
    j, v = place // 2, place % 2
    return (8 * v + j, 8 * v + 4 + j)


def nn(a, b):
    return lax.dot_general(a, b, (((1,), (0,)), ((), ())), preferred_element_type=F32)


def pack_kernel(k_ref, v_ref, q_ref, o_ref):
    rows = q_ref[...].astype(F32)
    for first, ref in ((0, k_ref), (144, v_ref)):
        turned = ref[...].astype(F32).T
        for place in range(8):
            a, b = heads_of(place)
            o_ref[place, first : first + 144, :] = jnp.concatenate(
                [turned[HD * a : HD * a + HD], turned[HD * b : HD * b + HD]], axis=0
            ).astype(BF)
    for place in range(8):
        a, b = heads_of(place)
        qa = rows[:, HD * a : HD * a + HD]
        qb = rows[:, HD * b : HD * b + HD]
        middle = jnp.concatenate([qa[16:24], qb[0:8]], axis=0)
        o_ref[place, 288:304, :] = jnp.concatenate(
            [qa[0:16], middle, qb[8:24], jnp.zeros((16, 40), F32)], axis=1
        ).astype(BF)


def weight_sum_kernel(v_ref, w_ref, keep_ref, send_ref):
    total = jnp.zeros((48, 256), F32)
    for source in range(16):
        total = total + w_ref[source].astype(F32)
    rows = jnp.concatenate([total[:, 72 * k : 72 * k + 72] for k in range(3)], axis=0)
    low, high = rows[:, 0:36], rows[:, 36:72]
    keep_ref[...] = jnp.where(v_ref[0] == 0, low, high)
    send_ref[...] = jnp.where(v_ref[0] == 0, high, low)


def scatter_kernel(v_ref, g_ref, keep_ref, come_ref, o_ref):
    heads = [None] * 16
    for place in range(8):
        piece = g_ref[place].astype(F32)
        tail = jnp.concatenate(
            [
                piece[96 + 8 * (g // 8) : 104 + 8 * (g // 8), 16 * (g % 8) : 16 * (g % 8) + 16]
                for g in range(12)
            ],
            axis=0,
        )
        a, b = heads_of(place)
        heads[a] = piece[0:96, 0:72]
        heads[b] = jnp.concatenate([piece[0:96, 72:128], tail], axis=1)
    rows = jnp.concatenate(heads, axis=1)
    for t in range(4):
        i = t % 2
        mine = keep_ref[HD * i : HD * i + HD, :]
        other = come_ref[HD * i : HD * i + HD, :]
        weight = jnp.where(v_ref[0] == t // 2, mine, other)
        folded = [weight[8 * k : 8 * k + 8] for k in range(9)] + [jnp.zeros((8, 828), F32)]
        o_ref[t] = jnp.concatenate(
            [rows[24 * t : 24 * t + 24], jnp.concatenate(folded, axis=1)], axis=0
        ).astype(BF)


def finish_kernel(x_ref, q_ref, w_ref):
    q_ref[...] = x_ref[0:24, :]
    folded = x_ref[...].astype(F32)[24:32]
    for k in range(9):
        w_ref[8 * k : 8 * k + 8, :] = folded[:, 36 * k : 36 * k + 36]


def unpack_kernel(g_ref, after_ref, k_ref, v_ref):
    for part, o_ref in ((0, k_ref), (1, v_ref)):
        heads = [None] * 16
        for place in range(8):
            block = g_ref[place, 144 * part : 144 * part + 144, :].astype(F32)
            a, b = heads_of(place)
            heads[a] = block[0:HD]
            heads[b] = block[HD : 2 * HD]
        o_ref[...] = jnp.concatenate(heads, axis=0).T.astype(BF)


def first_kernel(
    place_ref, kv_ref, qg_ref, keep_ref, come_ref, st_ref, ot_ref, q_ref, ga_ref, qs_ref, qt_ref
):
    step = pl.program_id(0)

    @pl.when(step == 0)
    def _():
        for block in range(32):
            piece = qg_ref[block].astype(F32)
            base = 24 * block
            qs_ref[0, base : base + 16, :] = piece[:, 0:72]
            qs_ref[0, base + 16 : base + 24, :] = piece[0:8, 72:144]
            qs_ref[1, base : base + 8, :] = piece[8:16, 72:144]
            qs_ref[1, base + 8 : base + 24, :] = piece[:, 144:216]
        @pl.when(place_ref[0] == 0)
        def _():
            ga_ref[:, :, 0:384] = keep_ref[...]
            ga_ref[:, :, 384:768] = come_ref[...]

        @pl.when(place_ref[0] == 1)
        def _():
            ga_ref[:, :, 0:384] = come_ref[...]
            ga_ref[:, :, 384:768] = keep_ref[...]

        for h in range(2):
            q_ref[h] = qs_ref[h].astype(BF)
            qt_ref[h] = qs_ref[h].T.astype(BF)
        st_ref[0:2, :] = jnp.full((2, ROWS), -1e30, F32)
        st_ref[2:8, :] = jnp.zeros((6, ROWS), F32)
        ot_ref[...] = jnp.zeros_like(ot_ref)

    keys = kv_ref[0, 0:144, :].astype(F32)
    values = kv_ref[0, 144:288, :].astype(F32)
    for h in range(2):
        kh = keys[HD * h : HD * h + HD].T.astype(BF)
        vt = values[HD * h : HD * h + HD]
        vh = vt.T.astype(BF)
        s = nn(kh, qt_ref[h])
        u = nn(vh, ga_ref[h])
        before = st_ref[h : h + 1, :]
        highest = jnp.maximum(before, jnp.max(s, axis=0, keepdims=True))
        again = jnp.exp2((before - highest) * SCALE)
        e = jnp.exp2((s - highest) * SCALE)
        st_ref[h : h + 1, :] = highest
        st_ref[2 + h : 3 + h, :] = st_ref[2 + h : 3 + h, :] * again + jnp.sum(
            e, axis=0, keepdims=True
        )
        st_ref[4 + h : 5 + h, :] = st_ref[4 + h : 5 + h, :] * again + jnp.sum(
            e * u, axis=0, keepdims=True
        )
        ot_ref[h] = ot_ref[h] * again + nn(vt.astype(BF), e.astype(BF))


def joined(sg_ref, h):
    tops = [sg_ref[t, h : h + 1, :] for t in range(4)]
    highest = jnp.maximum(jnp.maximum(tops[0], tops[1]), jnp.maximum(tops[2], tops[3]))
    total = jnp.zeros((1, ROWS), F32)
    weighted = jnp.zeros((1, ROWS), F32)
    for t in range(4):
        part = jnp.exp2((tops[t] - highest) * SCALE)
        total = total + sg_ref[t, 2 + h : 3 + h, :] * part
        weighted = weighted + sg_ref[t, 4 + h : 5 + h, :] * part
    return highest, total, weighted / total


def weight_kernel(sg_ref, st_ref, ot_ref, go_ref, o_ref):
    rows = []
    for h in range(2):
        highest, total, _ = joined(sg_ref, h)
        share = jnp.exp2((st_ref[h : h + 1, :] - highest) * SCALE) / total
        rows.append(ot_ref[h] * share)
    attn = jnp.concatenate(rows, axis=0).astype(BF)
    product = nn(attn, go_ref[...])
    for c in range(16):
        part = product[:, HD * c : HD * c + HD]
        o_ref[c] = jnp.concatenate(
            [part[0:48], part[48:96], part[96:144], jnp.zeros((48, 40), F32)], axis=1
        ).astype(BF)


def second_kernel(
    kv_ref, q_ref, ga_ref, sg_ref, after_ref, grad_ref, dq_ref, qt_ref, gn_ref, stat_ref, dqt_ref
):
    step = pl.program_id(0)

    @pl.when(step == 0)
    def _():
        for h in range(2):
            qt_ref[h] = q_ref[h].astype(F32).T.astype(BF)
            gn_ref[h] = ga_ref[h].astype(F32).T.astype(BF)
            highest, total, delta = joined(sg_ref, h)
            stat_ref[h : h + 1, :] = highest
            stat_ref[2 + h : 3 + h, :] = 1.0 / total
            stat_ref[4 + h : 5 + h, :] = delta
        dqt_ref[...] = jnp.zeros_like(dqt_ref)

    keys = kv_ref[0, 0:144, :].astype(F32)
    values = kv_ref[0, 144:288, :].astype(F32)
    dks, dvs = [], []
    for h in range(2):
        kt = keys[HD * h : HD * h + HD]
        kh = kt.T.astype(BF)
        vh = values[HD * h : HD * h + HD].T.astype(BF)
        s = nn(kh, qt_ref[h])
        u = nn(vh, ga_ref[h])
        p = jnp.exp2((s - stat_ref[h : h + 1, :]) * SCALE) * stat_ref[2 + h : 3 + h, :]
        ds = (p * (u - stat_ref[4 + h : 5 + h, :])).astype(BF)
        dvs.append(nn(p.astype(BF), gn_ref[h]).T)
        dks.append(nn(ds, q_ref[h]).T * FACTOR)
        dqt_ref[HD * h : HD * h + HD, :] += nn(kt.astype(BF), ds)
    grad_ref[0, 0:144, :] = jnp.concatenate(dks, axis=0).astype(BF)
    grad_ref[0, 144:288, :] = jnp.concatenate(dvs, axis=0).astype(BF)

    @pl.when(step == pl.num_programs(0) - 1)
    def _():
        rows = (dqt_ref[...] * FACTOR).T
        for s in range(8):
            own = [rows[192 * t + 24 * s : 192 * t + 24 * s + 24] for t in range(4)]
            tail = [own[g // 3][8 * (g % 3) : 8 * (g % 3) + 8, 128:144] for g in range(12)]
            tail = [
                jnp.concatenate(tail[0:8], axis=1),
                jnp.concatenate(tail[8:12] + [jnp.zeros((8, 64), F32)], axis=1),
            ]
            dq_ref[s] = jnp.concatenate([part[:, 0:128] for part in own] + tail, axis=0).astype(BF)


def whole(*shape):
    return pl.BlockSpec(shape, lambda i: (0,) * len(shape))


def block(*shape):
    return pl.BlockSpec((1,) + shape, lambda i: (i,) + (0,) * len(shape))


def on_device(slab_queries, key_tokens, value_tokens, grad_output, out_weight):
    query_rows = slab_queries[0]
    key_rows = key_tokens[0]
    value_rows = value_tokens[0]
    cotangent = grad_output[0]
    v = lax.axis_index("kv")
    swap = [(0, 1), (1, 0)]

    place = jnp.full((1,), v, jnp.int32)
    query_half = lax.dynamic_slice_in_dim(query_rows, 24 * v, 24, 0)
    packed = pl.pallas_call(
        pack_kernel,
        out_shape=jax.ShapeDtypeStruct((8, 304, 256), BF),
        compiler_params=PARAMS,
        name="pack_tokens",
    )(key_rows, value_rows, query_half)
    tokens = lax.all_to_all(packed, CUBE, 0, 0, tiled=True)

    cotangent_half = lax.dynamic_slice_in_dim(cotangent, 384 * v, 384, 0)
    grad_half = lax.dot_general(
        out_weight, cotangent_half, (((1,), (1,)), ((), ())), preferred_element_type=F32
    ).astype(BF)
    grad_four = lax.all_gather(grad_half, "t")
    grad_keep = lax.dynamic_slice_in_dim(grad_four, 2 * v, 2, 0)
    grad_sent = lax.dynamic_slice_in_dim(grad_four, 2 - 2 * v, 2, 0)
    grad_come = lax.ppermute(grad_sent, "kv", swap)

    query_pieces = lax.all_gather(tokens[:, 288:304, :].reshape(128, 256), "t")
    query_pieces = query_pieces.reshape(32, 16, 256)

    stats, attn_turned, queries, grad_heads = pl.pallas_call(
        first_kernel,
        grid=(8,),
        in_specs=[
            SCALAR,
            block(304, 256),
            whole(32, 16, 256),
            whole(2, HD, 384),
            whole(2, HD, 384),
        ],
        out_specs=[
            whole(8, ROWS),
            whole(2, HD, ROWS),
            whole(2, ROWS, HD),
            whole(2, HD, ROWS),
        ],
        out_shape=[
            jax.ShapeDtypeStruct((8, ROWS), F32),
            jax.ShapeDtypeStruct((2, HD, ROWS), F32),
            jax.ShapeDtypeStruct((2, ROWS, HD), BF),
            jax.ShapeDtypeStruct((2, HD, ROWS), BF),
        ],
        scratch_shapes=[pltpu.VMEM((2, ROWS, HD), F32), pltpu.VMEM((2, HD, ROWS), BF)],
        compiler_params=PARAMS_SEQ,
        name="first_pass",
    )(place, tokens, query_pieces, grad_keep, grad_come)

    gathered = lax.all_gather(stats, "t")

    weight_parts = pl.pallas_call(
        weight_kernel,
        out_shape=jax.ShapeDtypeStruct((16, 48, 256), BF),
        compiler_params=PARAMS,
        name="weight_part",
    )(gathered, stats, attn_turned, cotangent)
    weight_come = lax.all_to_all(weight_parts, DP, 0, 0, tiled=True)

    grads, query_grad = pl.pallas_call(
        second_kernel,
        grid=(8,),
        in_specs=[
            block(304, 256),
            whole(2, ROWS, HD),
            whole(2, HD, ROWS),
            whole(4, 8, ROWS),
            ANY,
        ],
        out_specs=[block(288, 256), whole(8, 112, 128)],
        out_shape=[
            jax.ShapeDtypeStruct((8, 288, 256), BF),
            jax.ShapeDtypeStruct((8, 112, 128), BF),
        ],
        scratch_shapes=[
            pltpu.VMEM((2, HD, ROWS), BF),
            pltpu.VMEM((2, ROWS, HD), BF),
            pltpu.VMEM((8, ROWS), F32),
            pltpu.VMEM((144, ROWS), F32),
        ],
        compiler_params=PARAMS_SEQ,
        name="second_pass",
    )(tokens, queries, grad_heads, gathered, weight_parts)

    query_come = lax.all_to_all(query_grad, CUBE, 0, 0, tiled=True)
    weight_keep, weight_sent = pl.pallas_call(
        weight_sum_kernel,
        out_shape=[jax.ShapeDtypeStruct((144, 36), F32)] * 2,
        in_specs=[SCALAR, HERE],
        compiler_params=PARAMS,
        name="weight_sum",
    )(place, weight_come)
    weight_other = lax.ppermute(weight_sent, "kv", swap)
    scattered = pl.pallas_call(
        scatter_kernel,
        out_shape=jax.ShapeDtypeStruct((4, 32, 1152), BF),
        in_specs=[SCALAR, HERE, HERE, HERE],
        compiler_params=PARAMS,
        name="scatter_pack",
    )(place, query_come, weight_keep, weight_other)
    summed = lax.psum_scatter(
        scattered.reshape(128, 1152), "t", scatter_dimension=0, tiled=True
    )
    query_out, weight_out = pl.pallas_call(
        finish_kernel,
        out_shape=[jax.ShapeDtypeStruct((24, 1152), BF), jax.ShapeDtypeStruct((HD, 36), F32)],
        compiler_params=PARAMS,
        cost_estimate=LONG,
        name="finish",
    )(summed)

    grads_back = lax.all_to_all(grads, CUBE, 0, 0, tiled=True)
    key_out, value_out = pl.pallas_call(
        unpack_kernel,
        out_shape=[jax.ShapeDtypeStruct((256, 1152), BF)] * 2,
        in_specs=[HERE, ANY],
        compiler_params=PARAMS,
        name="unpack_grads",
    )(grads_back, weight_out)
    return (key_out[None], value_out[None], query_out[None], weight_out)


def solution(mesh):
    cube = Mesh(mesh.devices.reshape(4, 2, 2, 4, 4, 2), DP + SEQ + ("kv",))
    return jax.shard_map(
        on_device,
        mesh=cube,
        in_specs=(
            P(DP, SEQ, None),
            P(DP, SEQ + ("kv",), None),
            P(DP, SEQ + ("kv",), None),
            P(DP, None, None),
            P(SEQ, None),
        ),
        out_specs=(
            P(DP, SEQ + ("kv",), None),
            P(DP, SEQ + ("kv",), None),
            P(DP, SEQ + ("kv",), None),
            P(SEQ, DP + ("kv",)),
        ),
        check_vma=False,
    )
```

```python
import math

import jax
import jax.numpy as jnp
from jax import lax
from jax.experimental import pallas as pl
from jax.experimental.pallas import tpu as pltpu
from jax.sharding import Mesh
from jax.sharding import PartitionSpec as P

HD = 72
ROWS = 768
FACTOR = 1.0 / math.sqrt(HD)
SCALE = FACTOR * math.log2(math.e)
BF = jnp.bfloat16
F32 = jnp.float32
VMEM = 60 * 1024 * 1024
LONG = pl.CostEstimate(flops=60_000_000_000, bytes_accessed=200_000_000, transcendentals=0)
ANY = pl.BlockSpec(memory_space=pl.ANY)
SCALAR = pl.BlockSpec(memory_space=pltpu.SMEM)
HERE = pl.BlockSpec(memory_space=pltpu.VMEM)
CUBE = ("j", "kv")
DP = ("y", "xh", "core")
SEQ = ("t", "j")
PARAMS = pltpu.CompilerParams(vmem_limit_bytes=VMEM)


def heads_of(place):
    j, v = place // 2, place % 2
    return (8 * v + j, 8 * v + 4 + j)


def nn(a, b):
    return lax.dot_general(a, b, (((1,), (0,)), ((), ())), preferred_element_type=F32)


def minus_parts(x):
    first = (-x).astype(BF)
    rest = -x - first.astype(F32)
    second = rest.astype(BF)
    third = (rest - second.astype(F32)).astype(BF)
    zeros = jnp.zeros((5,) + x.shape[1:], F32)
    return jnp.concatenate(
        [first.astype(F32), second.astype(F32), third.astype(F32), zeros], axis=0
    ).astype(BF)


def with_ones(x):
    row = lax.broadcasted_iota(jnp.int32, (8, x.shape[1]), 0)
    return jnp.concatenate([x, jnp.where(row < 3, 1.0, 0.0)], axis=0)


def pack_kernel(half_ref, k_ref, v_ref, q_ref, o_ref):
    every = q_ref[...].astype(F32)
    rows = jnp.where(half_ref[0] == 0, every[0:24], every[24:48])
    for first, ref in ((0, k_ref), (144, v_ref)):
        turned = ref[...].astype(F32).T
        for place in range(8):
            a, b = heads_of(place)
            o_ref[place, first : first + 144, :] = jnp.concatenate(
                [turned[HD * a : HD * a + HD], turned[HD * b : HD * b + HD]], axis=0
            ).astype(BF)
    for place in range(8):
        a, b = heads_of(place)
        qa = rows[:, HD * a : HD * a + HD]
        qb = rows[:, HD * b : HD * b + HD]
        middle = jnp.concatenate([qa[16:24], qb[0:8]], axis=0)
        o_ref[place, 288:304, :] = jnp.concatenate(
            [qa[0:16], middle, qb[8:24], jnp.zeros((16, 40), F32)], axis=1
        ).astype(BF)


def scatter_kernel(g_ref, w_ref, o_ref):
    heads = [None] * 16
    for place in range(8):
        piece = g_ref[place].astype(F32)
        tail = jnp.concatenate(
            [
                piece[96 + 8 * (g // 8) : 104 + 8 * (g // 8), 16 * (g % 8) : 16 * (g % 8) + 16]
                for g in range(12)
            ],
            axis=0,
        )
        a, b = heads_of(place)
        heads[a] = piece[0:96, 0:72]
        heads[b] = jnp.concatenate([piece[0:96, 72:128], tail], axis=1)
    rows = jnp.concatenate(heads, axis=1)
    for v in range(2):
        total = jnp.zeros((48, 128), F32)
        for source in range(16):
            total = total + w_ref[2 * source + v].astype(F32)
        weight = jnp.concatenate([total[:, 36 * k : 36 * k + 36] for k in range(3)], axis=0)
        for i in range(2):
            t = 2 * v + i
            folded = [weight[HD * i + 8 * k : HD * i + 8 * k + 8] for k in range(9)]
            folded = jnp.concatenate(folded + [jnp.zeros((8, 828), F32)], axis=1)
            o_ref[t] = jnp.concatenate([rows[24 * t : 24 * t + 24], folded], axis=0).astype(BF)


def finish_kernel(x_ref, q_ref, w_ref):
    q_ref[...] = x_ref[0:24, :]
    folded = x_ref[...].astype(F32)[24:32]
    weight = jnp.concatenate([folded[:, 36 * k : 36 * k + 36] for k in range(9)], axis=0)
    w_ref[...] = weight.T


def unpack_kernel(g_ref, after_ref, k_ref, v_ref):
    for part, o_ref in ((0, k_ref), (1, v_ref)):
        heads = [None] * 16
        for place in range(8):
            block = g_ref[place, 144 * part : 144 * part + 144, :].astype(F32)
            a, b = heads_of(place)
            heads[a] = block[0:HD]
            heads[b] = block[HD : 2 * HD]
        o_ref[...] = jnp.concatenate(heads, axis=0).T.astype(BF)


def first_kernel(
    half_ref, kv_ref, qg_ref, keep_ref, come_ref, st_ref, ot_ref, q_ref, ga_ref, qs_ref, qt_ref, kh_ref
):
    for block in range(32):
        piece = qg_ref[block].astype(F32)
        base = 24 * block
        qs_ref[0, base : base + 16, :] = piece[:, 0:72]
        qs_ref[0, base + 16 : base + 24, :] = piece[0:8, 72:144]
        qs_ref[1, base : base + 8, :] = piece[8:16, 72:144]
        qs_ref[1, base + 8 : base + 24, :] = piece[:, 144:216]

    @pl.when(half_ref[0] == 0)
    def _():
        ga_ref[:, :, 0:384] = keep_ref[...]
        ga_ref[:, :, 384:768] = come_ref[...]

    @pl.when(half_ref[0] == 1)
    def _():
        ga_ref[:, :, 0:384] = come_ref[...]
        ga_ref[:, :, 384:768] = keep_ref[...]

    for h in range(2):
        q_ref[h] = qs_ref[h].astype(BF)
        qt_ref[h, 0:72] = qs_ref[h].T.astype(BF)
    st_ref[0:2, :] = jnp.full((2, ROWS), -1e30, F32)
    st_ref[2:8, :] = jnp.zeros((6, ROWS), F32)
    ot_ref[...] = jnp.zeros_like(ot_ref)

    for i in range(8):
        keys = kv_ref[i, 0:144, :].astype(F32)
        for h in range(2):
            kh = with_ones(keys[HD * h : HD * h + HD]).T.astype(BF)
            kh_ref[h, i] = kh
            s = nn(kh[:, 0:72], qt_ref[h, 0:72])
            st_ref[h : h + 1, :] = jnp.maximum(
                st_ref[h : h + 1, :], jnp.max(s, axis=0, keepdims=True)
            )
    for h in range(2):
        qt_ref[h, 72:80] = minus_parts(st_ref[h : h + 1, :])
    for i in range(8):
        values = kv_ref[i, 144:288, :].astype(F32)
        for h in range(2):
            vt = values[HD * h : HD * h + HD]
            u = nn(vt.T.astype(BF), ga_ref[h])
            e = jnp.exp2(nn(kh_ref[h, i], qt_ref[h]) * SCALE)
            st_ref[2 + h : 3 + h, :] += jnp.sum(e, axis=0, keepdims=True)
            st_ref[4 + h : 5 + h, :] += jnp.sum(e * u, axis=0, keepdims=True)
            ot_ref[h] += nn(vt.astype(BF), e.astype(BF))


def joined(sg_ref, h):
    tops = [sg_ref[t, h : h + 1, :] for t in range(4)]
    highest = jnp.maximum(jnp.maximum(tops[0], tops[1]), jnp.maximum(tops[2], tops[3]))
    total = jnp.zeros((1, ROWS), F32)
    weighted = jnp.zeros((1, ROWS), F32)
    for t in range(4):
        part = jnp.exp2((tops[t] - highest) * SCALE)
        total = total + sg_ref[t, 2 + h : 3 + h, :] * part
        weighted = weighted + sg_ref[t, 4 + h : 5 + h, :] * part
    return highest, total, weighted / total


def weight_kernel(sg_ref, st_ref, ot_ref, go_ref, o_ref):
    rows = []
    for h in range(2):
        highest, total, _ = joined(sg_ref, h)
        share = jnp.exp2((st_ref[h : h + 1, :] - highest) * SCALE) / total
        rows.append(ot_ref[h] * share)
    attn = jnp.concatenate(rows, axis=0).astype(BF)
    product = nn(attn, go_ref[...])
    for c in range(32):
        part = product[:, 36 * c : 36 * c + 36]
        o_ref[c] = jnp.concatenate(
            [part[0:48], part[48:96], part[96:144], jnp.zeros((48, 20), F32)], axis=1
        ).astype(BF)


def second_kernel(
    kv_ref, q_ref, ga_ref, sg_ref, after_ref, grad_ref, dq_ref, qt_ref, gt_ref, gn_ref, dqt_ref
):
    for h in range(2):
        highest, total, delta = joined(sg_ref, h)
        level = highest + jnp.log2(total) * (1.0 / SCALE)
        qt_ref[h, 0:72] = q_ref[h].astype(F32).T.astype(BF)
        qt_ref[h, 72:80] = minus_parts(level)
        grads = ga_ref[h].astype(F32)
        gt_ref[h, 0:72] = ga_ref[h]
        gt_ref[h, 72:80] = minus_parts(delta)
        gn_ref[h] = grads.T.astype(BF)
    dqt_ref[...] = jnp.zeros_like(dqt_ref)

    for i in range(8):
        keys = kv_ref[i, 0:144, :].astype(F32)
        values = kv_ref[i, 144:288, :].astype(F32)
        dks, dvs = [], []
        for h in range(2):
            kt = keys[HD * h : HD * h + HD]
            kh = with_ones(kt).T.astype(BF)
            vh = with_ones(values[HD * h : HD * h + HD]).T.astype(BF)
            p = jnp.exp2(nn(kh, qt_ref[h]) * SCALE)
            ds = (p * nn(vh, gt_ref[h])).astype(BF)
            dvs.append(nn(p.astype(BF), gn_ref[h]).T)
            dks.append(nn(ds, q_ref[h]).T * FACTOR)
            dqt_ref[HD * h : HD * h + HD, :] += nn(kt.astype(BF), ds)
        grad_ref[i, 0:144, :] = jnp.concatenate(dks, axis=0).astype(BF)
        grad_ref[i, 144:288, :] = jnp.concatenate(dvs, axis=0).astype(BF)

    rows = (dqt_ref[...] * FACTOR).T
    for s in range(8):
        own = [rows[192 * t + 24 * s : 192 * t + 24 * s + 24] for t in range(4)]
        tail = [own[g // 3][8 * (g % 3) : 8 * (g % 3) + 8, 128:144] for g in range(12)]
        tail = [
            jnp.concatenate(tail[0:8], axis=1),
            jnp.concatenate(tail[8:12] + [jnp.zeros((8, 64), F32)], axis=1),
        ]
        dq_ref[s] = jnp.concatenate([part[:, 0:128] for part in own] + tail, axis=0).astype(BF)


def on_device(slab_queries, key_tokens, value_tokens, grad_output, out_weight):
    query_rows = slab_queries[0]
    key_rows = key_tokens[0]
    value_rows = value_tokens[0]
    cotangent = grad_output[0]
    v = lax.axis_index("kv")
    swap = [(0, 1), (1, 0)]

    place = jnp.full((1,), v, jnp.int32)
    packed = pl.pallas_call(
        pack_kernel,
        out_shape=jax.ShapeDtypeStruct((8, 304, 256), BF),
        in_specs=[SCALAR, HERE, HERE, HERE],
        compiler_params=PARAMS,
        name="pack_tokens",
    )(place, key_rows, value_rows, query_rows)
    tokens = lax.all_to_all(packed, CUBE, 0, 0, tiled=True)

    cotangent_half = lax.dynamic_slice_in_dim(cotangent, 384 * v, 384, 0)
    grad_half = lax.dot_general(
        out_weight, cotangent_half, (((1,), (1,)), ((), ())), preferred_element_type=F32
    ).astype(BF)
    grad_four = lax.all_gather(grad_half, "t")
    grad_keep = lax.dynamic_slice_in_dim(grad_four, 2 * v, 2, 0)
    grad_sent = lax.dynamic_slice_in_dim(grad_four, 2 - 2 * v, 2, 0)
    grad_come = lax.ppermute(grad_sent, "kv", swap)

    query_pieces = lax.all_gather(tokens[:, 288:304, :].reshape(128, 256), "t")
    query_pieces = query_pieces.reshape(32, 16, 256)

    stats, attn_turned, queries, grad_heads = pl.pallas_call(
        first_kernel,
        in_specs=[SCALAR, HERE, HERE, HERE, HERE],
        out_shape=[
            jax.ShapeDtypeStruct((8, ROWS), F32),
            jax.ShapeDtypeStruct((2, HD, ROWS), F32),
            jax.ShapeDtypeStruct((2, ROWS, HD), BF),
            jax.ShapeDtypeStruct((2, HD, ROWS), BF),
        ],
        scratch_shapes=[
            pltpu.VMEM((2, ROWS, HD), F32),
            pltpu.VMEM((2, 80, ROWS), BF),
            pltpu.VMEM((2, 8, 256, 80), BF),
        ],
        compiler_params=PARAMS,
        name="first_pass",
    )(place, tokens, query_pieces, grad_keep, grad_come)

    gathered = lax.all_gather(stats, "t")

    weight_parts = pl.pallas_call(
        weight_kernel,
        out_shape=jax.ShapeDtypeStruct((32, 48, 128), BF),
        compiler_params=PARAMS,
        name="weight_part",
    )(gathered, stats, attn_turned, cotangent)
    weight_come = lax.all_to_all(weight_parts, DP + ("kv",), 0, 0, tiled=True)

    grads, query_grad = pl.pallas_call(
        second_kernel,
        in_specs=[HERE, HERE, HERE, HERE, ANY],
        out_shape=[
            jax.ShapeDtypeStruct((8, 288, 256), BF),
            jax.ShapeDtypeStruct((8, 112, 128), BF),
        ],
        scratch_shapes=[
            pltpu.VMEM((2, 80, ROWS), BF),
            pltpu.VMEM((2, 80, ROWS), BF),
            pltpu.VMEM((2, ROWS, HD), BF),
            pltpu.VMEM((144, ROWS), F32),
        ],
        compiler_params=PARAMS,
        name="second_pass",
    )(tokens, queries, grad_heads, gathered, weight_parts)

    query_come = lax.all_to_all(query_grad, CUBE, 0, 0, tiled=True)
    scattered = pl.pallas_call(
        scatter_kernel,
        out_shape=jax.ShapeDtypeStruct((4, 32, 1152), BF),
        compiler_params=PARAMS,
        name="scatter_pack",
    )(query_come, weight_come)
    summed = lax.psum_scatter(
        scattered.reshape(128, 1152), "t", scatter_dimension=0, tiled=True
    )
    query_out, weight_out = pl.pallas_call(
        finish_kernel,
        out_shape=[jax.ShapeDtypeStruct((24, 1152), BF), jax.ShapeDtypeStruct((36, HD), F32)],
        compiler_params=PARAMS,
        cost_estimate=LONG,
        name="finish",
    )(summed)

    grads_back = lax.all_to_all(grads, CUBE, 0, 0, tiled=True)
    key_out, value_out = pl.pallas_call(
        unpack_kernel,
        out_shape=[jax.ShapeDtypeStruct((256, 1152), BF)] * 2,
        in_specs=[HERE, ANY],
        compiler_params=PARAMS,
        name="unpack_grads",
    )(grads_back, weight_out)
    return (key_out[None], value_out[None], query_out[None], weight_out.T)


def solution(mesh):
    cube = Mesh(mesh.devices.reshape(4, 2, 2, 4, 4, 2), DP + SEQ + ("kv",))
    return jax.shard_map(
        on_device,
        mesh=cube,
        in_specs=(
            P(DP, SEQ, None),
            P(DP, SEQ + ("kv",), None),
            P(DP, SEQ + ("kv",), None),
            P(DP, None, None),
            P(SEQ, None),
        ),
        out_specs=(
            P(DP, SEQ + ("kv",), None),
            P(DP, SEQ + ("kv",), None),
            P(DP, SEQ + ("kv",), None),
            P(SEQ, DP + ("kv",)),
        ),
        check_vma=False,
    )
```

```python
import math

import jax
import jax.numpy as jnp
from jax import lax
from jax.experimental import pallas as pl
from jax.experimental.pallas import tpu as pltpu
from jax.sharding import Mesh
from jax.sharding import PartitionSpec as P

HD = 72
ROWS = 768
FACTOR = 1.0 / math.sqrt(HD)
SCALE = FACTOR * math.log2(math.e)
BF = jnp.bfloat16
F32 = jnp.float32
VMEM = 24 * 1024 * 1024
LONG = pl.CostEstimate(flops=60_000_000_000, bytes_accessed=200_000_000, transcendentals=0)
ANY = pl.BlockSpec(memory_space=pl.ANY)
SCALAR = pl.BlockSpec(memory_space=pltpu.SMEM)
HERE = pl.BlockSpec(memory_space=pltpu.VMEM)
CUBE = ("j", "kv")
DP = ("y", "xh", "core")
SEQ = ("t", "j")
PARAMS = pltpu.CompilerParams(vmem_limit_bytes=VMEM)


def heads_of(place):
    j, v = place // 2, place % 2
    return (8 * v + j, 8 * v + 4 + j)


def nn(a, b):
    return lax.dot_general(a, b, (((1,), (0,)), ((), ())), preferred_element_type=F32)


def minus_parts(x):
    first = (-x).astype(BF)
    rest = -x - first.astype(F32)
    second = rest.astype(BF)
    third = (rest - second.astype(F32)).astype(BF)
    zeros = jnp.zeros((5,) + x.shape[1:], F32)
    return jnp.concatenate(
        [first.astype(F32), second.astype(F32), third.astype(F32), zeros], axis=0
    ).astype(BF)


def with_ones(x):
    row = lax.broadcasted_iota(jnp.int32, (8, x.shape[1]), 0)
    return jnp.concatenate([x, jnp.where(row < 3, 1.0, 0.0)], axis=0)


def pack_heads(ref, o_ref):
    turned = ref[...].astype(F32).T
    for place in range(8):
        a, b = heads_of(place)
        o_ref[place, 0:144, :] = jnp.concatenate(
            [turned[HD * a : HD * a + HD], turned[HD * b : HD * b + HD]], axis=0
        ).astype(BF)


def pack_keys_kernel(half_ref, k_ref, q_ref, o_ref):
    pack_heads(k_ref, o_ref)
    every = q_ref[...].astype(F32)
    rows = jnp.where(half_ref[0] == 0, every[0:24], every[24:48])
    for place in range(8):
        a, b = heads_of(place)
        qa = rows[:, HD * a : HD * a + HD]
        qb = rows[:, HD * b : HD * b + HD]
        middle = jnp.concatenate([qa[16:24], qb[0:8]], axis=0)
        o_ref[place, 144:160, :] = jnp.concatenate(
            [qa[0:16], middle, qb[8:24], jnp.zeros((16, 40), F32)], axis=1
        ).astype(BF)


def scatter_kernel(g_ref, w_ref, o_ref):
    heads = [None] * 16
    for place in range(8):
        piece = g_ref[place].astype(F32)
        tail = jnp.concatenate(
            [
                piece[96 + 8 * (g // 8) : 104 + 8 * (g // 8), 16 * (g % 8) : 16 * (g % 8) + 16]
                for g in range(12)
            ],
            axis=0,
        )
        a, b = heads_of(place)
        heads[a] = piece[0:96, 0:72]
        heads[b] = jnp.concatenate([piece[0:96, 72:128], tail], axis=1)
    rows = jnp.concatenate(heads, axis=1)
    for v in range(2):
        total = jnp.zeros((48, 128), F32)
        for source in range(16):
            total = total + w_ref[2 * source + v].astype(F32)
        weight = jnp.concatenate([total[:, 36 * k : 36 * k + 36] for k in range(3)], axis=0)
        for i in range(2):
            t = 2 * v + i
            folded = [weight[HD * i + 24 * k : HD * i + 24 * k + 24] for k in range(3)]
            own = rows[24 * t : 24 * t + 24]
            o_ref[t] = jnp.concatenate([own] + folded + [jnp.zeros((24, 20), F32)], axis=1).astype(BF)


def finish_kernel(x_ref, q_ref, w_ref):
    q_ref[...] = x_ref[:, 0:1152]
    folded = x_ref[:, 1152:1280].astype(F32)
    weight = jnp.concatenate([folded[:, 36 * k : 36 * k + 36] for k in range(3)], axis=0)
    w_ref[...] = weight.T


def unpack_kernel(g_ref, after_ref, k_ref, v_ref, held_ref, sems):
    copies = []
    for part in range(2):
        copies.append(
            pltpu.make_async_copy(
                g_ref.at[:, pl.ds(144 * part, 144), :], held_ref.at[part], sems.at[part]
            )
        )
        copies[part].start()
    for part, o_ref in ((0, k_ref), (1, v_ref)):
        copies[part].wait()
        heads = [None] * 16
        for place in range(8):
            block = held_ref[part, place].astype(F32)
            a, b = heads_of(place)
            heads[a] = block[0:HD]
            heads[b] = block[HD : 2 * HD]
        o_ref[...] = jnp.concatenate(heads, axis=0).T.astype(BF)


def first_kernel(
    half_ref,
    k_ref,
    v_ref,
    qg_ref,
    keep_ref,
    come_ref,
    st_ref,
    ot_ref,
    q_ref,
    ga_ref,
    qs_ref,
    qt_ref,
    s_ref,
):
    for block in range(32):
        piece = qg_ref[block].astype(F32)
        base = 24 * block
        qs_ref[0, base : base + 16, :] = piece[:, 0:72]
        qs_ref[0, base + 16 : base + 24, :] = piece[0:8, 72:144]
        qs_ref[1, base : base + 8, :] = piece[8:16, 72:144]
        qs_ref[1, base + 8 : base + 24, :] = piece[:, 144:216]

    @pl.when(half_ref[0] == 0)
    def _():
        ga_ref[:, :, 0:384] = keep_ref[...]
        ga_ref[:, :, 384:768] = come_ref[...]

    @pl.when(half_ref[0] == 1)
    def _():
        ga_ref[:, :, 0:384] = come_ref[...]
        ga_ref[:, :, 384:768] = keep_ref[...]

    for h in range(2):
        q_ref[h] = qs_ref[h].astype(BF)
        qt_ref[h] = qs_ref[h].T.astype(BF)

    tops = [None, None]
    for i in range(8):
        keys = k_ref[i, 0:144, :].astype(F32)
        for h in range(2):
            s = nn(keys[HD * h : HD * h + HD].T.astype(BF), qt_ref[h])
            s_ref[h, i] = s
            top = jnp.max(s, axis=0, keepdims=True)
            tops[h] = top if i == 0 else jnp.maximum(tops[h], top)

    totals = [jnp.zeros((1, ROWS), F32)] * 2
    weighted = [jnp.zeros((1, ROWS), F32)] * 2
    ot_ref[...] = jnp.zeros_like(ot_ref)
    for i in range(8):
        values = v_ref[i].astype(F32)
        for h in range(2):
            vt = values[HD * h : HD * h + HD]
            u = nn(vt.T.astype(BF), ga_ref[h])
            e = jnp.exp2((s_ref[h, i] - tops[h]) * SCALE)
            totals[h] = totals[h] + jnp.sum(e, axis=0, keepdims=True)
            weighted[h] = weighted[h] + jnp.sum(e * u, axis=0, keepdims=True)
            ot_ref[h] += nn(vt.astype(BF), e.astype(BF))
    rest = jnp.zeros((2, ROWS), F32)
    st_ref[...] = jnp.concatenate(tops + totals + weighted + [rest], axis=0)


def joined(sg_ref, h):
    tops = [sg_ref[t, h : h + 1, :] for t in range(4)]
    highest = jnp.maximum(jnp.maximum(tops[0], tops[1]), jnp.maximum(tops[2], tops[3]))
    total = jnp.zeros((1, ROWS), F32)
    weighted = jnp.zeros((1, ROWS), F32)
    for t in range(4):
        part = jnp.exp2((tops[t] - highest) * SCALE)
        total = total + sg_ref[t, 2 + h : 3 + h, :] * part
        weighted = weighted + sg_ref[t, 4 + h : 5 + h, :] * part
    return highest, total, weighted / total


def weight_kernel(sg_ref, st_ref, ot_ref, go_ref, o_ref):
    rows = []
    for h in range(2):
        highest, total, _ = joined(sg_ref, h)
        share = jnp.exp2((st_ref[h : h + 1, :] - highest) * SCALE) / total
        rows.append(ot_ref[h] * share)
    attn = jnp.concatenate(rows, axis=0).astype(BF)
    product = nn(attn, go_ref[...])
    for c in range(32):
        part = product[:, 36 * c : 36 * c + 36]
        o_ref[c] = jnp.concatenate(
            [part[0:48], part[48:96], part[96:144], jnp.zeros((48, 20), F32)], axis=1
        ).astype(BF)


def second_kernel(
    k_ref, v_ref, q_ref, ga_ref, sg_ref, after_ref, grad_ref, dq_ref, qt_ref, gt_ref, gn_ref, dqt_ref
):
    for h in range(2):
        highest, total, delta = joined(sg_ref, h)
        level = highest + jnp.log2(total) * (1.0 / SCALE)
        qt_ref[h, 0:72] = q_ref[h].astype(F32).T.astype(BF)
        qt_ref[h, 72:80] = minus_parts(level)
        gt_ref[h, 0:72] = ga_ref[h]
        gt_ref[h, 72:80] = minus_parts(delta)
        gn_ref[h] = ga_ref[h].astype(F32).T.astype(BF)
    dqt_ref[...] = jnp.zeros_like(dqt_ref)

    for i in range(8):
        keys = k_ref[i, 0:144, :].astype(F32)
        values = v_ref[i].astype(F32)
        dks, dvs = [], []
        for h in range(2):
            kt = keys[HD * h : HD * h + HD]
            kh = with_ones(kt).T.astype(BF)
            vh = with_ones(values[HD * h : HD * h + HD]).T.astype(BF)
            p = jnp.exp2(nn(kh, qt_ref[h]) * SCALE)
            ds = (p * nn(vh, gt_ref[h])).astype(BF)
            dvs.append(nn(p.astype(BF), gn_ref[h]).T)
            dks.append(nn(ds, q_ref[h]).T * FACTOR)
            dqt_ref[HD * h : HD * h + HD, :] += nn(kt.astype(BF), ds)
        grad_ref[i, 0:144, :] = jnp.concatenate(dks, axis=0).astype(BF)
        grad_ref[i, 144:288, :] = jnp.concatenate(dvs, axis=0).astype(BF)

    rows = (dqt_ref[...] * FACTOR).T
    for s in range(8):
        own = [rows[192 * t + 24 * s : 192 * t + 24 * s + 24] for t in range(4)]
        tail = [own[g // 3][8 * (g % 3) : 8 * (g % 3) + 8, 128:144] for g in range(12)]
        tail = [
            jnp.concatenate(tail[0:8], axis=1),
            jnp.concatenate(tail[8:12] + [jnp.zeros((8, 64), F32)], axis=1),
        ]
        dq_ref[s] = jnp.concatenate([part[:, 0:128] for part in own] + tail, axis=0).astype(BF)


def on_device(slab_queries, key_tokens, value_tokens, grad_output, out_weight):
    query_rows = slab_queries[0]
    key_rows = key_tokens[0]
    value_rows = value_tokens[0]
    cotangent = grad_output[0]
    v = lax.axis_index("kv")
    swap = [(0, 1), (1, 0)]

    place = jnp.full((1,), v, jnp.int32)
    packed_keys = pl.pallas_call(
        pack_keys_kernel,
        out_shape=jax.ShapeDtypeStruct((8, 160, 256), BF),
        in_specs=[SCALAR, HERE, HERE],
        compiler_params=PARAMS,
        name="pack_keys",
    )(place, key_rows, query_rows)
    keys = lax.all_to_all(packed_keys, CUBE, 0, 0, tiled=True)
    packed_values = pl.pallas_call(
        pack_heads,
        out_shape=jax.ShapeDtypeStruct((8, 144, 256), BF),
        compiler_params=PARAMS,
        name="pack_values",
    )(value_rows)

    cotangent_half = lax.dynamic_slice_in_dim(cotangent, 384 * v, 384, 0)
    grad_half = lax.dot_general(
        out_weight, cotangent_half, (((1,), (1,)), ((), ())), preferred_element_type=F32
    ).astype(BF)
    grad_four = lax.all_gather(grad_half, "t")
    packed_values, grad_four = lax.optimization_barrier((packed_values, grad_four))
    values = lax.all_to_all(packed_values, CUBE, 0, 0, tiled=True)
    grad_keep = lax.dynamic_slice_in_dim(grad_four, 2 * v, 2, 0)
    grad_sent = lax.dynamic_slice_in_dim(grad_four, 2 - 2 * v, 2, 0)
    grad_come = lax.ppermute(grad_sent, "kv", swap)

    query_pieces = lax.all_gather(keys[:, 144:160, :].reshape(128, 256), "t")
    query_pieces = query_pieces.reshape(32, 16, 256)

    stats, attn_turned, queries, grad_heads = pl.pallas_call(
        first_kernel,
        in_specs=[SCALAR] + [HERE] * 5,
        out_shape=[
            jax.ShapeDtypeStruct((8, ROWS), F32),
            jax.ShapeDtypeStruct((2, HD, ROWS), F32),
            jax.ShapeDtypeStruct((2, ROWS, HD), BF),
            jax.ShapeDtypeStruct((2, HD, ROWS), BF),
        ],
        scratch_shapes=[
            pltpu.VMEM((2, ROWS, HD), F32),
            pltpu.VMEM((2, HD, ROWS), BF),
            pltpu.VMEM((2, 8, 256, ROWS), F32),
        ],
        compiler_params=PARAMS,
        name="first_pass",
    )(place, keys, values, query_pieces, grad_keep, grad_come)

    gathered = lax.all_gather(stats, "t")

    weight_parts = pl.pallas_call(
        weight_kernel,
        out_shape=jax.ShapeDtypeStruct((32, 48, 128), BF),
        compiler_params=PARAMS,
        name="weight_part",
    )(gathered, stats, attn_turned, cotangent)
    weight_come = lax.all_to_all(weight_parts, DP + ("kv",), 0, 0, tiled=True)

    grads, query_grad = pl.pallas_call(
        second_kernel,
        in_specs=[HERE] * 5 + [ANY],
        out_shape=[
            jax.ShapeDtypeStruct((8, 288, 256), BF),
            jax.ShapeDtypeStruct((8, 112, 128), BF),
        ],
        scratch_shapes=[
            pltpu.VMEM((2, 80, ROWS), BF),
            pltpu.VMEM((2, 80, ROWS), BF),
            pltpu.VMEM((2, ROWS, HD), BF),
            pltpu.VMEM((144, ROWS), F32),
        ],
        compiler_params=PARAMS,
        name="second_pass",
    )(keys, values, queries, grad_heads, gathered, weight_parts)

    query_come = lax.all_to_all(query_grad, CUBE, 0, 0, tiled=True)
    scattered = pl.pallas_call(
        scatter_kernel,
        out_shape=jax.ShapeDtypeStruct((4, 24, 1280), BF),
        compiler_params=PARAMS,
        name="scatter_pack",
    )(query_come, weight_come)
    summed = lax.psum_scatter(
        scattered.reshape(96, 1280), "t", scatter_dimension=0, tiled=True
    )
    query_out, weight_out = pl.pallas_call(
        finish_kernel,
        out_shape=[jax.ShapeDtypeStruct((24, 1152), BF), jax.ShapeDtypeStruct((36, HD), F32)],
        compiler_params=PARAMS,
        cost_estimate=LONG,
        name="finish",
    )(summed)

    grads_back = lax.all_to_all(grads, CUBE, 0, 0, tiled=True)
    key_out, value_out = pl.pallas_call(
        unpack_kernel,
        out_shape=[jax.ShapeDtypeStruct((256, 1152), BF)] * 2,
        in_specs=[pl.BlockSpec(memory_space=pltpu.HBM), ANY],
        scratch_shapes=[pltpu.VMEM((2, 8, 144, 256), BF), pltpu.SemaphoreType.DMA((2,))],
        compiler_params=PARAMS,
        name="unpack_grads",
    )(grads_back, weight_out)
    return (key_out[None], value_out[None], query_out[None], weight_out.T)


def solution(mesh):
    cube = Mesh(mesh.devices.reshape(4, 2, 2, 4, 4, 2), DP + SEQ + ("kv",))
    return jax.shard_map(
        on_device,
        mesh=cube,
        in_specs=(
            P(DP, SEQ, None),
            P(DP, SEQ + ("kv",), None),
            P(DP, SEQ + ("kv",), None),
            P(DP, None, None),
            P(SEQ, None),
        ),
        out_specs=(
            P(DP, SEQ + ("kv",), None),
            P(DP, SEQ + ("kv",), None),
            P(DP, SEQ + ("kv",), None),
            P(SEQ, DP + ("kv",)),
        ),
        check_vma=False,
    )
```

```python
import math

import jax
import jax.numpy as jnp
from jax import lax
from jax.experimental import pallas as pl
from jax.experimental.pallas import tpu as pltpu
from jax.sharding import Mesh
from jax.sharding import PartitionSpec as P

HD = 72
ROWS = 768
FACTOR = 1.0 / math.sqrt(HD)
SCALE = FACTOR * math.log2(math.e)
BF = jnp.bfloat16
F32 = jnp.float32
VMEM = 24 * 1024 * 1024
LONG = pl.CostEstimate(flops=60_000_000_000, bytes_accessed=200_000_000, transcendentals=0)
ANY = pl.BlockSpec(memory_space=pl.ANY)
SCALAR = pl.BlockSpec(memory_space=pltpu.SMEM)
HERE = pl.BlockSpec(memory_space=pltpu.VMEM)
CUBE = ("j", "kv")
DP = ("y", "xh", "core")
SEQ = ("t", "j")
PARAMS = pltpu.CompilerParams(vmem_limit_bytes=VMEM)


def heads_of(place):
    j, v = place // 2, place % 2
    return (8 * v + j, 8 * v + 4 + j)


def nn(a, b):
    return lax.dot_general(a, b, (((1,), (0,)), ((), ())), preferred_element_type=F32)


def minus_parts(x):
    first = (-x).astype(BF)
    rest = -x - first.astype(F32)
    second = rest.astype(BF)
    third = (rest - second.astype(F32)).astype(BF)
    zeros = jnp.zeros((5,) + x.shape[1:], F32)
    return jnp.concatenate(
        [first.astype(F32), second.astype(F32), third.astype(F32), zeros], axis=0
    ).astype(BF)


def with_ones(x):
    row = lax.broadcasted_iota(jnp.int32, (8, x.shape[1]), 0)
    return jnp.concatenate([x, jnp.where(row < 3, 1.0, 0.0)], axis=0)


def pack_heads(ref, o_ref):
    turned = ref[...].astype(F32).T
    for place in range(8):
        a, b = heads_of(place)
        o_ref[place, 0:144, :] = jnp.concatenate(
            [turned[HD * a : HD * a + HD], turned[HD * b : HD * b + HD]], axis=0
        ).astype(BF)


def pack_keys_kernel(half_ref, k_ref, q_ref, o_ref):
    pack_heads(k_ref, o_ref)
    every = q_ref[...].astype(F32)
    rows = jnp.where(half_ref[0] == 0, every[0:24], every[24:48])
    for place in range(8):
        a, b = heads_of(place)
        qa = rows[:, HD * a : HD * a + HD]
        qb = rows[:, HD * b : HD * b + HD]
        middle = jnp.concatenate([qa[16:24], qb[0:8]], axis=0)
        o_ref[place, 144:160, :] = jnp.concatenate(
            [qa[0:16], middle, qb[8:24], jnp.zeros((16, 40), F32)], axis=1
        ).astype(BF)


def scatter_kernel(g_ref, w_ref, o_ref):
    heads = [None] * 16
    for place in range(8):
        piece = g_ref[place].astype(F32)
        tail = jnp.concatenate(
            [
                piece[96 + 8 * (g // 8) : 104 + 8 * (g // 8), 16 * (g % 8) : 16 * (g % 8) + 16]
                for g in range(12)
            ],
            axis=0,
        )
        a, b = heads_of(place)
        heads[a] = piece[0:96, 0:72]
        heads[b] = jnp.concatenate([piece[0:96, 72:128], tail], axis=1)
    rows = jnp.concatenate(heads, axis=1)
    for v in range(2):
        total = jnp.zeros((48, 128), F32)
        for source in range(16):
            total = total + w_ref[2 * source + v].astype(F32)
        weight = jnp.concatenate([total[:, 36 * k : 36 * k + 36] for k in range(3)], axis=0)
        for i in range(2):
            t = 2 * v + i
            folded = [weight[HD * i + 24 * k : HD * i + 24 * k + 24] for k in range(3)]
            own = rows[24 * t : 24 * t + 24]
            o_ref[t] = jnp.concatenate([own] + folded + [jnp.zeros((24, 20), F32)], axis=1).astype(BF)


def finish_kernel(x_ref, q_ref, w_ref):
    q_ref[...] = x_ref[:, 0:1152]
    folded = x_ref[:, 1152:1280].astype(F32)
    weight = jnp.concatenate([folded[:, 36 * k : 36 * k + 36] for k in range(3)], axis=0)
    w_ref[...] = weight.T


def unpack_kernel(g_ref, k_ref, v_ref, held_ref, sems):
    copies = []
    for part in range(2):
        copies.append(
            pltpu.make_async_copy(
                g_ref.at[:, pl.ds(144 * part, 144), :], held_ref.at[part], sems.at[part]
            )
        )
        copies[part].start()
    for part, o_ref in ((0, k_ref), (1, v_ref)):
        copies[part].wait()
        heads = [None] * 16
        for place in range(8):
            block = held_ref[part, place].astype(F32)
            a, b = heads_of(place)
            heads[a] = block[0:HD]
            heads[b] = block[HD : 2 * HD]
        o_ref[...] = jnp.concatenate(heads, axis=0).T.astype(BF)


def rows_of(qg_ref, qs_ref):
    for block in range(32):
        piece = qg_ref[block].astype(F32)
        base = 24 * block
        qs_ref[0, base : base + 16, :] = piece[:, 0:72]
        qs_ref[0, base + 16 : base + 24, :] = piece[0:8, 72:144]
        qs_ref[1, base : base + 8, :] = piece[8:16, 72:144]
        qs_ref[1, base + 8 : base + 24, :] = piece[:, 144:216]


def first_kernel(k_ref, v_ref, qg_ref, ga_ref, st_ref, ot_ref, qs_ref, qt_ref, s_ref):
    rows_of(qg_ref, qs_ref)
    for h in range(2):
        qt_ref[h] = qs_ref[h].T.astype(BF)

    tops = [None, None]
    for i in range(8):
        keys = k_ref[i, 0:144, :].astype(F32)
        for h in range(2):
            s = nn(keys[HD * h : HD * h + HD].T.astype(BF), qt_ref[h])
            s_ref[h, i] = s
            top = jnp.max(s, axis=0, keepdims=True)
            tops[h] = top if i == 0 else jnp.maximum(tops[h], top)

    totals = [jnp.zeros((1, ROWS), F32)] * 2
    weighted = [jnp.zeros((1, ROWS), F32)] * 2
    ot_ref[...] = jnp.zeros_like(ot_ref)
    for i in range(8):
        values = v_ref[i].astype(F32)
        for h in range(2):
            vt = values[HD * h : HD * h + HD]
            u = nn(vt.T.astype(BF), ga_ref[h])
            e = jnp.exp2((s_ref[h, i] - tops[h]) * SCALE)
            totals[h] = totals[h] + jnp.sum(e, axis=0, keepdims=True)
            weighted[h] = weighted[h] + jnp.sum(e * u, axis=0, keepdims=True)
            ot_ref[h] += nn(vt.astype(BF), e.astype(BF))
    rest = jnp.zeros((2, ROWS), F32)
    st_ref[...] = jnp.concatenate(tops + totals + weighted + [rest], axis=0)


def joined(sg_ref, h):
    tops = [sg_ref[t, h : h + 1, :] for t in range(4)]
    highest = jnp.maximum(jnp.maximum(tops[0], tops[1]), jnp.maximum(tops[2], tops[3]))
    total = jnp.zeros((1, ROWS), F32)
    weighted = jnp.zeros((1, ROWS), F32)
    for t in range(4):
        part = jnp.exp2((tops[t] - highest) * SCALE)
        total = total + sg_ref[t, 2 + h : 3 + h, :] * part
        weighted = weighted + sg_ref[t, 4 + h : 5 + h, :] * part
    return highest, total, weighted / total


def weight_kernel(sg_ref, st_ref, ot_ref, go_ref, o_ref):
    rows = []
    for h in range(2):
        highest, total, _ = joined(sg_ref, h)
        share = jnp.exp2((st_ref[h : h + 1, :] - highest) * SCALE) / total
        rows.append(ot_ref[h] * share)
    attn = jnp.concatenate(rows, axis=0).astype(BF)
    product = nn(attn, go_ref[...])
    for c in range(32):
        part = product[:, 36 * c : 36 * c + 36]
        o_ref[c] = jnp.concatenate(
            [part[0:48], part[48:96], part[96:144], jnp.zeros((48, 20), F32)], axis=1
        ).astype(BF)


def second_kernel(
    k_ref, v_ref, qg_ref, ga_ref, sg_ref, grad_ref, dq_ref, qs_ref, q_ref, qt_ref, gt_ref, gn_ref, dqt_ref
):
    rows_of(qg_ref, qs_ref)
    for h in range(2):
        highest, total, delta = joined(sg_ref, h)
        level = highest + jnp.log2(total) * (1.0 / SCALE)
        q_ref[h] = qs_ref[h].astype(BF)
        qt_ref[h, 0:72] = qs_ref[h].T.astype(BF)
        qt_ref[h, 72:80] = minus_parts(level)
        gt_ref[h, 0:72] = ga_ref[h]
        gt_ref[h, 72:80] = minus_parts(delta)
        gn_ref[h] = ga_ref[h].astype(F32).T.astype(BF)
    dqt_ref[...] = jnp.zeros_like(dqt_ref)

    for i in range(8):
        keys = k_ref[i, 0:144, :].astype(F32)
        values = v_ref[i].astype(F32)
        dks, dvs = [], []
        for h in range(2):
            kt = keys[HD * h : HD * h + HD]
            kh = with_ones(kt).T.astype(BF)
            vh = with_ones(values[HD * h : HD * h + HD]).T.astype(BF)
            p = jnp.exp2(nn(kh, qt_ref[h]) * SCALE)
            ds = (p * nn(vh, gt_ref[h])).astype(BF)
            dvs.append(nn(p.astype(BF), gn_ref[h]).T)
            dks.append(nn(ds, q_ref[h]).T * FACTOR)
            dqt_ref[HD * h : HD * h + HD, :] += nn(kt.astype(BF), ds)
        grad_ref[i, 0:144, :] = jnp.concatenate(dks, axis=0).astype(BF)
        grad_ref[i, 144:288, :] = jnp.concatenate(dvs, axis=0).astype(BF)

    rows = (dqt_ref[...] * FACTOR).T
    for s in range(8):
        own = [rows[192 * t + 24 * s : 192 * t + 24 * s + 24] for t in range(4)]
        tail = [own[g // 3][8 * (g % 3) : 8 * (g % 3) + 8, 128:144] for g in range(12)]
        tail = [
            jnp.concatenate(tail[0:8], axis=1),
            jnp.concatenate(tail[8:12] + [jnp.zeros((8, 64), F32)], axis=1),
        ]
        dq_ref[s] = jnp.concatenate([part[:, 0:128] for part in own] + tail, axis=0).astype(BF)


def on_device(slab_queries, key_tokens, value_tokens, grad_output, out_weight):
    query_rows = slab_queries[0]
    key_rows = key_tokens[0]
    value_rows = value_tokens[0]
    cotangent = grad_output[0]
    v = lax.axis_index("kv")
    swap = [(0, 1), (1, 0)]

    place = jnp.full((1,), v, jnp.int32)
    packed_keys = pl.pallas_call(
        pack_keys_kernel,
        out_shape=jax.ShapeDtypeStruct((8, 160, 256), BF),
        in_specs=[SCALAR, HERE, HERE],
        compiler_params=pltpu.CompilerParams(vmem_limit_bytes=60 * 1024 * 1024),
        name="pack_keys",
    )(place, key_rows, query_rows)
    keys = lax.all_to_all(packed_keys, CUBE, 0, 0, tiled=True)
    packed_values = pl.pallas_call(
        pack_heads,
        out_shape=jax.ShapeDtypeStruct((8, 144, 256), BF),
        compiler_params=PARAMS,
        name="pack_values",
    )(value_rows)

    cotangent_half = lax.dynamic_slice_in_dim(cotangent, 384 * v, 384, 0)
    grad_half = lax.dot_general(
        out_weight, cotangent_half, (((1,), (1,)), ((), ())), preferred_element_type=F32
    ).astype(BF)
    grad_four = lax.all_gather(grad_half, "t")
    packed_values, grad_four = lax.optimization_barrier((packed_values, grad_four))
    values = lax.all_to_all(packed_values, CUBE, 0, 0, tiled=True)
    grad_keep = lax.dynamic_slice_in_dim(grad_four, 2 * v, 2, 0)
    grad_sent = lax.dynamic_slice_in_dim(grad_four, 2 - 2 * v, 2, 0)
    grad_come = lax.ppermute(grad_sent, "kv", swap)

    query_pieces = lax.all_gather(keys[:, 144:160, :].reshape(128, 256), "t")
    query_pieces = query_pieces.reshape(32, 16, 256)

    grad_heads = jnp.where(
        v == 0,
        jnp.concatenate([grad_keep, grad_come], axis=2),
        jnp.concatenate([grad_come, grad_keep], axis=2),
    )
    stats, attn_turned = pl.pallas_call(
        first_kernel,
        out_shape=[
            jax.ShapeDtypeStruct((8, ROWS), F32),
            jax.ShapeDtypeStruct((2, HD, ROWS), F32),
        ],
        scratch_shapes=[
            pltpu.VMEM((2, ROWS, HD), F32),
            pltpu.VMEM((2, HD, ROWS), BF),
            pltpu.VMEM((2, 8, 256, ROWS), F32),
        ],
        compiler_params=PARAMS,
        name="first_pass",
    )(keys, values, query_pieces, grad_heads)

    gathered = lax.all_gather(stats, "t")

    weight_parts = pl.pallas_call(
        weight_kernel,
        out_shape=jax.ShapeDtypeStruct((32, 48, 128), BF),
        compiler_params=PARAMS,
        name="weight_part",
    )(gathered, stats, attn_turned, cotangent)
    weight_come = lax.all_to_all(weight_parts, DP + ("kv",), 0, 0, tiled=True)

    gathered, weight_parts = lax.optimization_barrier((gathered, weight_parts))
    grads, query_grad = pl.pallas_call(
        second_kernel,
        out_shape=[
            jax.ShapeDtypeStruct((8, 288, 256), BF),
            jax.ShapeDtypeStruct((8, 112, 128), BF),
        ],
        scratch_shapes=[
            pltpu.VMEM((2, ROWS, HD), F32),
            pltpu.VMEM((2, ROWS, HD), BF),
            pltpu.VMEM((2, 80, ROWS), BF),
            pltpu.VMEM((2, 80, ROWS), BF),
            pltpu.VMEM((2, ROWS, HD), BF),
            pltpu.VMEM((144, ROWS), F32),
        ],
        compiler_params=PARAMS,
        name="second_pass",
    )(keys, values, query_pieces, grad_heads, gathered)

    query_come = lax.all_to_all(query_grad, CUBE, 0, 0, tiled=True)
    scattered = pl.pallas_call(
        scatter_kernel,
        out_shape=jax.ShapeDtypeStruct((4, 24, 1280), BF),
        compiler_params=PARAMS,
        name="scatter_pack",
    )(query_come, weight_come)
    summed = lax.psum_scatter(
        scattered.reshape(96, 1280), "t", scatter_dimension=0, tiled=True
    )
    query_out, weight_out = pl.pallas_call(
        finish_kernel,
        out_shape=[jax.ShapeDtypeStruct((24, 1152), BF), jax.ShapeDtypeStruct((36, HD), F32)],
        compiler_params=PARAMS,
        cost_estimate=LONG,
        name="finish",
    )(summed)

    grads_back = lax.all_to_all(grads, CUBE, 0, 0, tiled=True)
    key_out, value_out = pl.pallas_call(
        unpack_kernel,
        out_shape=[jax.ShapeDtypeStruct((256, 1152), BF)] * 2,
        in_specs=[pl.BlockSpec(memory_space=pl.ANY)],
        scratch_shapes=[pltpu.VMEM((2, 8, 144, 256), BF), pltpu.SemaphoreType.DMA((2,))],
        compiler_params=PARAMS,
        name="unpack_grads",
    )(grads_back)
    return (key_out[None], value_out[None], query_out[None], weight_out.T)


def solution(mesh):
    cube = Mesh(mesh.devices.reshape(4, 2, 2, 4, 4, 2), DP + SEQ + ("kv",))
    return jax.shard_map(
        on_device,
        mesh=cube,
        in_specs=(
            P(DP, SEQ, None),
            P(DP, SEQ + ("kv",), None),
            P(DP, SEQ + ("kv",), None),
            P(DP, None, None),
            P(SEQ, None),
        ),
        out_specs=(
            P(DP, SEQ + ("kv",), None),
            P(DP, SEQ + ("kv",), None),
            P(DP, SEQ + ("kv",), None),
            P(SEQ, DP + ("kv",)),
        ),
        check_vma=False,
    )
```

```python
import math

import jax
import jax.numpy as jnp
from jax import lax
from jax.experimental import pallas as pl
from jax.experimental.pallas import tpu as pltpu
from jax.sharding import Mesh
from jax.sharding import PartitionSpec as P

HD = 72
ROWS = 768
FACTOR = 1.0 / math.sqrt(HD)
SCALE = FACTOR * math.log2(math.e)
BF = jnp.bfloat16
F32 = jnp.float32
VMEM = 24 * 1024 * 1024
ANY = pl.BlockSpec(memory_space=pl.ANY)
SCALAR = pl.BlockSpec(memory_space=pltpu.SMEM)
HERE = pl.BlockSpec(memory_space=pltpu.VMEM)
CUBE = ("j", "kv")
DP = ("y", "xh", "core")
SEQ = ("t", "j")
PARAMS = pltpu.CompilerParams(vmem_limit_bytes=VMEM)


def heads_of(place):
    j, v = place // 2, place % 2
    return (8 * v + j, 8 * v + 4 + j)


def nn(a, b):
    return lax.dot_general(a, b, (((1,), (0,)), ((), ())), preferred_element_type=F32)


def minus_parts(x):
    first = (-x).astype(BF)
    rest = -x - first.astype(F32)
    second = rest.astype(BF)
    third = (rest - second.astype(F32)).astype(BF)
    zeros = jnp.zeros((5,) + x.shape[1:], F32)
    return jnp.concatenate(
        [first.astype(F32), second.astype(F32), third.astype(F32), zeros], axis=0
    ).astype(BF)


def with_ones(x):
    row = lax.broadcasted_iota(jnp.int32, (8, x.shape[1]), 0)
    return jnp.concatenate([x, jnp.where(row < 3, 1.0, 0.0)], axis=0)


def pack_heads(ref, o_ref):
    turned = ref[...].astype(F32).T
    for place in range(8):
        a, b = heads_of(place)
        o_ref[place, 0:144, :] = jnp.concatenate(
            [turned[HD * a : HD * a + HD], turned[HD * b : HD * b + HD]], axis=0
        ).astype(BF)


def pack_keys_kernel(half_ref, k_ref, q_ref, o_ref):
    pack_heads(k_ref, o_ref)
    every = q_ref[...].astype(F32)
    rows = jnp.where(half_ref[0] == 0, every[0:24], every[24:48])
    for place in range(8):
        a, b = heads_of(place)
        qa = rows[:, HD * a : HD * a + HD]
        qb = rows[:, HD * b : HD * b + HD]
        middle = jnp.concatenate([qa[16:24], qb[0:8]], axis=0)
        o_ref[place, 144:160, :] = jnp.concatenate(
            [qa[0:16], middle, qb[8:24], jnp.zeros((16, 40), F32)], axis=1
        ).astype(BF)


def scatter_kernel(g_ref, w_ref, o_ref):
    heads = [None] * 16
    for place in range(8):
        piece = g_ref[place].astype(F32)
        tail = jnp.concatenate(
            [
                piece[96 + 8 * (g // 8) : 104 + 8 * (g // 8), 16 * (g % 8) : 16 * (g % 8) + 16]
                for g in range(12)
            ],
            axis=0,
        )
        a, b = heads_of(place)
        heads[a] = piece[0:96, 0:72]
        heads[b] = jnp.concatenate([piece[0:96, 72:128], tail], axis=1)
    rows = jnp.concatenate(heads, axis=1)
    for v in range(2):
        total = jnp.zeros((48, 128), F32)
        for source in range(16):
            total = total + w_ref[2 * source + v].astype(F32)
        weight = jnp.concatenate([total[:, 36 * k : 36 * k + 36] for k in range(3)], axis=0)
        for i in range(2):
            t = 2 * v + i
            folded = [weight[HD * i + 24 * k : HD * i + 24 * k + 24] for k in range(3)]
            own = rows[24 * t : 24 * t + 24]
            o_ref[t] = jnp.concatenate([own] + folded + [jnp.zeros((24, 20), F32)], axis=1).astype(BF)


def finish_kernel(x_ref, q_ref, w_ref):
    q_ref[...] = x_ref[:, 0:1152]
    folded = x_ref[:, 1152:1280].astype(F32)
    weight = jnp.concatenate([folded[:, 36 * k : 36 * k + 36] for k in range(3)], axis=0)
    w_ref[...] = weight.T


def unpack_kernel(g_ref, k_ref, v_ref, held_ref, sems):
    copies = []
    for part in range(2):
        copies.append(
            pltpu.make_async_copy(
                g_ref.at[:, pl.ds(144 * part, 144), :], held_ref.at[part], sems.at[part]
            )
        )
        copies[part].start()
    for part, o_ref in ((0, k_ref), (1, v_ref)):
        copies[part].wait()
        heads = [None] * 16
        for place in range(8):
            block = held_ref[part, place].astype(F32)
            a, b = heads_of(place)
            heads[a] = block[0:HD]
            heads[b] = block[HD : 2 * HD]
        o_ref[...] = jnp.concatenate(heads, axis=0).T.astype(BF)


def rows_of(qg_ref, qs_ref):
    for block in range(32):
        piece = qg_ref[block].astype(F32)
        base = 24 * block
        qs_ref[0, base : base + 16, :] = piece[:, 0:72]
        qs_ref[0, base + 16 : base + 24, :] = piece[0:8, 72:144]
        qs_ref[1, base : base + 8, :] = piece[8:16, 72:144]
        qs_ref[1, base + 8 : base + 24, :] = piece[:, 144:216]


def first_kernel(k_ref, v_ref, qg_ref, ga_ref, st_ref, ot_ref, qs_ref, qt_ref, s_ref):
    rows_of(qg_ref, qs_ref)
    for h in range(2):
        qt_ref[h] = qs_ref[h].T.astype(BF)

    tops = [None, None]
    for i in range(8):
        keys = k_ref[i, 0:144, :].astype(F32)
        for h in range(2):
            s = nn(keys[HD * h : HD * h + HD].T.astype(BF), qt_ref[h])
            s_ref[h, i] = s
            top = jnp.max(s, axis=0, keepdims=True)
            tops[h] = top if i == 0 else jnp.maximum(tops[h], top)

    totals = [jnp.zeros((1, ROWS), F32)] * 2
    weighted = [jnp.zeros((1, ROWS), F32)] * 2
    ot_ref[...] = jnp.zeros_like(ot_ref)
    for i in range(8):
        values = v_ref[i].astype(F32)
        for h in range(2):
            vt = values[HD * h : HD * h + HD]
            u = nn(vt.T.astype(BF), ga_ref[h])
            e = jnp.exp2((s_ref[h, i] - tops[h]) * SCALE)
            totals[h] = totals[h] + jnp.sum(e, axis=0, keepdims=True)
            weighted[h] = weighted[h] + jnp.sum(e * u, axis=0, keepdims=True)
            ot_ref[h] += nn(vt.astype(BF), e.astype(BF))
    rest = jnp.zeros((2, ROWS), F32)
    st_ref[...] = jnp.concatenate(tops + totals + weighted + [rest], axis=0)


def joined(sg_ref, h):
    tops = [sg_ref[t, h : h + 1, :] for t in range(4)]
    highest = jnp.maximum(jnp.maximum(tops[0], tops[1]), jnp.maximum(tops[2], tops[3]))
    total = jnp.zeros((1, ROWS), F32)
    weighted = jnp.zeros((1, ROWS), F32)
    for t in range(4):
        part = jnp.exp2((tops[t] - highest) * SCALE)
        total = total + sg_ref[t, 2 + h : 3 + h, :] * part
        weighted = weighted + sg_ref[t, 4 + h : 5 + h, :] * part
    return highest, total, weighted / total


def weight_kernel(sg_ref, st_ref, ot_ref, go_ref, o_ref):
    rows = []
    for h in range(2):
        highest, total, _ = joined(sg_ref, h)
        share = jnp.exp2((st_ref[h : h + 1, :] - highest) * SCALE) / total
        rows.append(ot_ref[h] * share)
    attn = jnp.concatenate(rows, axis=0).astype(BF)
    product = nn(attn, go_ref[...])
    for c in range(32):
        part = product[:, 36 * c : 36 * c + 36]
        o_ref[c] = jnp.concatenate(
            [part[0:48], part[48:96], part[96:144], jnp.zeros((48, 20), F32)], axis=1
        ).astype(BF)


def second_kernel(
    k_ref, v_ref, qg_ref, ga_ref, sg_ref, grad_ref, dq_ref, qs_ref, q_ref, qt_ref, gt_ref, gn_ref, dqt_ref
):
    rows_of(qg_ref, qs_ref)
    for h in range(2):
        highest, total, delta = joined(sg_ref, h)
        level = highest + jnp.log2(total) * (1.0 / SCALE)
        q_ref[h] = qs_ref[h].astype(BF)
        qt_ref[h, 0:72] = qs_ref[h].T.astype(BF)
        qt_ref[h, 72:80] = minus_parts(level)
        gt_ref[h, 0:72] = ga_ref[h]
        gt_ref[h, 72:80] = minus_parts(delta)
        gn_ref[h] = ga_ref[h].astype(F32).T.astype(BF)
    dqt_ref[...] = jnp.zeros_like(dqt_ref)

    for i in range(8):
        keys = k_ref[i, 0:144, :].astype(F32)
        values = v_ref[i].astype(F32)
        dks, dvs = [], []
        for h in range(2):
            kt = keys[HD * h : HD * h + HD]
            kh = with_ones(kt).T.astype(BF)
            vh = with_ones(values[HD * h : HD * h + HD]).T.astype(BF)
            p = jnp.exp2(nn(kh, qt_ref[h]) * SCALE)
            ds = (p * nn(vh, gt_ref[h])).astype(BF)
            dvs.append(nn(p.astype(BF), gn_ref[h]).T)
            dks.append(nn(ds, q_ref[h]).T * FACTOR)
            dqt_ref[HD * h : HD * h + HD, :] += nn(kt.astype(BF), ds)
        grad_ref[i, 0:144, :] = jnp.concatenate(dks, axis=0).astype(BF)
        grad_ref[i, 144:288, :] = jnp.concatenate(dvs, axis=0).astype(BF)

    rows = (dqt_ref[...] * FACTOR).T
    for s in range(8):
        own = [rows[192 * t + 24 * s : 192 * t + 24 * s + 24] for t in range(4)]
        tail = [own[g // 3][8 * (g % 3) : 8 * (g % 3) + 8, 128:144] for g in range(12)]
        tail = [
            jnp.concatenate(tail[0:8], axis=1),
            jnp.concatenate(tail[8:12] + [jnp.zeros((8, 64), F32)], axis=1),
        ]
        dq_ref[s] = jnp.concatenate([part[:, 0:128] for part in own] + tail, axis=0).astype(BF)


def on_device(slab_queries, key_tokens, value_tokens, grad_output, out_weight):
    query_rows = slab_queries[0]
    key_rows = key_tokens[0]
    value_rows = value_tokens[0]
    cotangent = grad_output[0]
    v = lax.axis_index("kv")
    swap = [(0, 1), (1, 0)]

    place = jnp.full((1,), v, jnp.int32)
    packed_keys = pl.pallas_call(
        pack_keys_kernel,
        out_shape=jax.ShapeDtypeStruct((8, 160, 256), BF),
        in_specs=[SCALAR, HERE, HERE],
        compiler_params=pltpu.CompilerParams(vmem_limit_bytes=60 * 1024 * 1024),
        name="pack_keys",
    )(place, key_rows, query_rows)
    keys = lax.all_to_all(packed_keys, CUBE, 0, 0, tiled=True)
    packed_values = pl.pallas_call(
        pack_heads,
        out_shape=jax.ShapeDtypeStruct((8, 144, 256), BF),
        compiler_params=PARAMS,
        name="pack_values",
    )(value_rows)

    cotangent_half = lax.dynamic_slice_in_dim(cotangent, 384 * v, 384, 0)
    grad_half = lax.dot_general(
        out_weight, cotangent_half, (((1,), (1,)), ((), ())), preferred_element_type=F32
    ).astype(BF)
    grad_four = lax.all_gather(grad_half, "t")
    packed_values, grad_four = lax.optimization_barrier((packed_values, grad_four))
    values = lax.all_to_all(packed_values, CUBE, 0, 0, tiled=True)
    grad_keep = lax.dynamic_slice_in_dim(grad_four, 2 * v, 2, 0)
    grad_sent = lax.dynamic_slice_in_dim(grad_four, 2 - 2 * v, 2, 0)
    grad_come = lax.ppermute(grad_sent, "kv", swap)

    query_pieces = lax.all_gather(keys[:, 144:160, :].reshape(128, 256), "t")
    query_pieces = query_pieces.reshape(32, 16, 256)

    grad_heads = jnp.where(
        v == 0,
        jnp.concatenate([grad_keep, grad_come], axis=2),
        jnp.concatenate([grad_come, grad_keep], axis=2),
    )
    stats, attn_turned = pl.pallas_call(
        first_kernel,
        out_shape=[
            jax.ShapeDtypeStruct((8, ROWS), F32),
            jax.ShapeDtypeStruct((2, HD, ROWS), F32),
        ],
        scratch_shapes=[
            pltpu.VMEM((2, ROWS, HD), F32),
            pltpu.VMEM((2, HD, ROWS), BF),
            pltpu.VMEM((2, 8, 256, ROWS), F32),
        ],
        compiler_params=PARAMS,
        name="first_pass",
    )(keys, values, query_pieces, grad_heads)

    gathered = lax.all_gather(stats, "t")

    weight_parts = pl.pallas_call(
        weight_kernel,
        out_shape=jax.ShapeDtypeStruct((32, 48, 128), BF),
        compiler_params=PARAMS,
        name="weight_part",
    )(gathered, stats, attn_turned, cotangent)
    weight_come = lax.all_to_all(weight_parts, DP + ("kv",), 0, 0, tiled=True)

    gathered, weight_parts = lax.optimization_barrier((gathered, weight_parts))
    grads, query_grad = pl.pallas_call(
        second_kernel,
        out_shape=[
            jax.ShapeDtypeStruct((8, 288, 256), BF),
            jax.ShapeDtypeStruct((8, 112, 128), BF),
        ],
        scratch_shapes=[
            pltpu.VMEM((2, ROWS, HD), F32),
            pltpu.VMEM((2, ROWS, HD), BF),
            pltpu.VMEM((2, 80, ROWS), BF),
            pltpu.VMEM((2, 80, ROWS), BF),
            pltpu.VMEM((2, ROWS, HD), BF),
            pltpu.VMEM((144, ROWS), F32),
        ],
        compiler_params=PARAMS,
        name="second_pass",
    )(keys, values, query_pieces, grad_heads, gathered)

    query_come = lax.all_to_all(query_grad, CUBE, 0, 0, tiled=True)
    scattered = pl.pallas_call(
        scatter_kernel,
        out_shape=jax.ShapeDtypeStruct((4, 24, 1280), BF),
        compiler_params=PARAMS,
        name="scatter_pack",
    )(query_come, weight_come)
    summed = lax.psum_scatter(
        scattered.reshape(96, 1280), "t", scatter_dimension=0, tiled=True
    )
    grads_back = lax.all_to_all(grads, CUBE, 0, 0, tiled=True)
    key_out, value_out = pl.pallas_call(
        unpack_kernel,
        out_shape=[jax.ShapeDtypeStruct((256, 1152), BF)] * 2,
        in_specs=[pl.BlockSpec(memory_space=pl.ANY)],
        scratch_shapes=[pltpu.VMEM((2, 8, 144, 256), BF), pltpu.SemaphoreType.DMA((2,))],
        compiler_params=PARAMS,
        name="unpack_grads",
    )(grads_back)
    summed, key_out = lax.optimization_barrier((summed, key_out))
    query_out, weight_out = pl.pallas_call(
        finish_kernel,
        out_shape=[jax.ShapeDtypeStruct((24, 1152), BF), jax.ShapeDtypeStruct((36, HD), F32)],
        compiler_params=PARAMS,
        name="finish",
    )(summed)
    return (key_out[None], value_out[None], query_out[None], weight_out.T)


def solution(mesh):
    cube = Mesh(mesh.devices.reshape(4, 2, 2, 4, 4, 2), DP + SEQ + ("kv",))
    return jax.shard_map(
        on_device,
        mesh=cube,
        in_specs=(
            P(DP, SEQ, None),
            P(DP, SEQ + ("kv",), None),
            P(DP, SEQ + ("kv",), None),
            P(DP, None, None),
            P(SEQ, None),
        ),
        out_specs=(
            P(DP, SEQ + ("kv",), None),
            P(DP, SEQ + ("kv",), None),
            P(DP, SEQ + ("kv",), None),
            P(SEQ, DP + ("kv",)),
        ),
        check_vma=False,
    )
```
